32 devices in a mesh: ctx: 8 (over z, x), tp: 4 (over y, core).
Axes of the slice: x: 2, y: 2, z: 4, core: 2. Of those that a mesh axis runs over, the one named last changes fastest.
Arguments:
- projected: bfloat16 [1024, 3, 4096], P('ctx', None, 'tp'), may hold values from -6 to 6
- short_filter: float32 [7, 3, 4096], P(None, None, 'tp'), may hold values from -2.4 to 2.4
- long_filter: bfloat16 [256, 512], P('tp'), may hold values from -0.53033009 to 0.53033009
- out_weight: bfloat16 [4096, 8192], P('tp'), may hold values from -0.09375 to 0.09375
Outputs:
- layer_out: bfloat16 [1024, 8192], P('ctx', 'tp')
The draws below stay inside these ranges and needn't reach their ends.
All inputs are finite; a program needn't handle non-finite values.
Results may differ from the reference program's by a relative error of at most 0.015.
Values may be sent and summed in bfloat16 or wider, within the bound.
A program may use at most 64 MiB of HBM per device.

```python
import math
import jax
import jax.numpy as jnp
from jax import lax

C = 4096
DOUT = 8192
GSIZE = 16
TAPS = 7
TOKENS = 1024
FILT = 512
GROUPS = 256
N_TP = 4


def draw_long_filter(key, part):
    key_rate = jax.random.fold_in(key, 11)
    key_noise = jax.random.fold_in(key, 12)
    rates = jnp.exp(jax.random.uniform(key_rate, (GROUPS, 1), jnp.float32, math.log(0.2), math.log(4.0)))
    position = jnp.arange(FILT, dtype=jnp.float32)[None, :] / FILT
    envelope = jnp.exp(-rates * position) * jnp.sqrt(2.0 * rates / FILT / (1.0 - jnp.exp(-2.0 * rates)))
    noise = jnp.clip(jax.random.normal(key_noise, (GROUPS, FILT), jnp.float32), -4.0, 4.0)
    return (noise * envelope).astype(jnp.bfloat16)


def block_scale(key, dims, pieces, low, high):
    gain, own = 1.0, jax.random.fold_in(key, 6)
    for dim, parts in pieces:
        heights = jnp.exp(jax.random.uniform(jax.random.fold_in(own, dim), (parts,), jnp.float32, low / len(pieces), high / len(pieces)))
        gain = gain * jnp.repeat(heights, dims[dim] // parts).reshape([-1 if axis == dim else 1 for axis in range(len(dims))])
    return gain


def bell_draw(own_key, dims, spread, limit, shards=(), held_as=jnp.bfloat16):
    array = spread * jax.random.normal(own_key, dims, jnp.float32)
    if shards:
        array = array * block_scale(own_key, dims, shards, -0.22, 0.18)
    return jnp.clip(array, -limit, limit).astype(held_as)


def setup_inputs(seed: int = 0) -> dict:
    streams_of = jax.random.split(jax.random.key(seed), 5)
    return {
        "projected": bell_draw(streams_of[0], (TOKENS, 3, C), 1.0, 6.0, ((0, 8), (2, 4))),
        "short_filter": bell_draw(streams_of[1], (TAPS, 3, C), 0.4, 2.4, ((2, 4),), jnp.float32),
        "long_filter": draw_long_filter(jax.random.fold_in(streams_of[4], 71), 0),
        "out_weight": bell_draw(streams_of[3], (C, DOUT), C ** -0.5, 0.09375, ((0, 4),)),
    }


def reference(projected, short_filter, long_filter, out_weight):
    features = projected.astype(jnp.float32)
    padded = jnp.pad(features, ((TAPS - 1, 0), (0, 0), (0, 0)))
    conved = short_filter[0] * padded[TAPS - 1:TAPS - 1 + TOKENS]
    for offset in range(1, TAPS):
        conved = conved + short_filter[offset] * padded[TAPS - 1 - offset:TAPS - 1 - offset + TOKENS]
    values = (conved[:, 1, :] * conved[:, 2, :]).astype(jnp.bfloat16)
    channel_taps = jnp.repeat(long_filter.astype(jnp.float32), GSIZE, axis=0).T
    length = 2 * TOKENS
    spectrum = jnp.fft.rfft(values.astype(jnp.float32), n=length, axis=0) * jnp.fft.rfft(channel_taps, n=length, axis=0)
    mixed = jnp.fft.irfft(spectrum, n=length, axis=0)[:TOKENS]
    hidden = (conved[:, 0, :] * mixed).astype(jnp.bfloat16)
    share = C // N_TP
    total = jnp.zeros((TOKENS, DOUT), jnp.float32)
    for group in range(N_TP):
        partial_sum = jnp.dot(hidden[:, group * share:(group + 1) * share], out_weight[group * share:(group + 1) * share], preferred_element_type=jnp.float32)
        rounded = lax.optimization_barrier(partial_sum.astype(jnp.bfloat16))
        total = total + rounded.astype(jnp.float32)
    return total.astype(jnp.bfloat16)
```

```python
import functools

import jax
import jax.numpy as jnp
from jax import lax
from jax.experimental import pallas as pl
from jax.experimental.pallas import tpu as pltpu
from jax.sharding import PartitionSpec as P

GSIZE = 16
EDGE = 16


def aligned(start, size):
    return pl.ds(pl.multiple_of(start, size), size)


def fused_kernel(
    lanes,
    cores_y,
    proj,
    short,
    longf,
    weight,
    out,
    held_weight,
    border,
    padded,
    toeplitz,
    gate,
    send_v,
    recv_v,
    send_m,
    recv_m,
    hidden,
    core_send,
    core_recv,
    y_send,
    y_recv,
    w_sem,
    edge_sem,
    v_sems,
    v_recvs,
    m_sems,
    m_recvs,
    cs_sems,
    cr_sems,
    ys_sems,
    yr_sems,
):
    me = lax.axis_index("ctx")
    tp = lax.axis_index("tp")
    y, core = tp // 2, tp % 2
    partner = y * 2 + (1 - core)
    _, rows, chans = proj.shape
    taps = short.shape[0]
    reach = longf.shape[1]
    behind = reach // rows
    share = chans // lanes
    own_groups = share // GSIZE
    pieces, wide = y_send.shape[1], y_send.shape[3]

    load = pltpu.make_async_copy(weight, held_weight, w_sem)
    load.start()

    barrier = pltpu.get_barrier_semaphore()
    for k in range(1, lanes):
        pl.semaphore_signal(barrier, inc=1, device_id={"ctx": lax.rem(me + k, lanes)})
    pl.semaphore_signal(barrier, inc=1, device_id={"tp": partner})
    for dy in range(1, cores_y):
        pl.semaphore_signal(
            barrier, inc=1, device_id={"tp": lax.rem(y + dy, cores_y) * 2 + core}
        )
    pl.semaphore_wait(barrier, lanes - 1 + 1 + cores_y - 1)

    edge = pltpu.make_async_remote_copy(
        src_ref=proj.at[:, pl.ds(rows - EDGE, EDGE), :],
        dst_ref=border,
        send_sem=edge_sem.at[0],
        recv_sem=edge_sem.at[1],
        device_id={"ctx": lax.rem(me + 1, lanes)},
    )
    edge.start()

    groups = longf.shape[0]
    padded[:, 0:rows] = jnp.zeros((groups, rows), jnp.float32)
    padded[:, rows : rows + reach] = longf[...].astype(jnp.float32)
    padded[:, rows + reach :] = jnp.zeros((groups, rows), jnp.float32)
    recv_v[0:behind] = jnp.zeros((behind, share, rows), jnp.bfloat16)

    def build(g, _):
        line = padded[pl.ds(me * own_groups + g, 1), :]
        flat = jnp.broadcast_to(line, (rows, reach + 2 * rows))
        skewed = pltpu.roll(flat, 0, 1, stride=1, stride_axis=0)
        for b in range(behind + 1):
            low = rows + reach - rows * b
            toeplitz[g, b * rows : (b + 1) * rows, :] = skewed[:, low : low + rows].astype(jnp.bfloat16)
        return 0

    lax.fori_loop(0, own_groups, build, 0)
    edge.wait()

    def conv(p, j):
        cols = aligned(j * share, share)
        before = jnp.where(me == 0, 0.0, border[p, :, cols].astype(jnp.float32))
        ext = jnp.concatenate([before, proj[p, :, cols].astype(jnp.float32)], axis=0)
        total = short[0, p : p + 1, cols] * ext[EDGE:]
        for d in range(1, taps):
            total = total + short[d, p : p + 1, cols] * pltpu.roll(ext, d, 0)[EDGE:]
        return total

    def values_of(j):
        return (conv(1, j) * conv(2, j)).T.astype(jnp.bfloat16)

    def values_copy(slot, peer):
        return pltpu.make_async_remote_copy(
            src_ref=send_v.at[peer],
            dst_ref=recv_v.at[behind + slot],
            send_sem=v_sems.at[peer],
            recv_sem=v_recvs.at[slot],
            device_id={"ctx": peer},
        )

    def mixed_copy(slot, peer):
        return pltpu.make_async_remote_copy(
            src_ref=send_m.at[peer],
            dst_ref=recv_m.at[slot],
            send_sem=m_sems.at[peer],
            recv_sem=m_recvs.at[slot],
            device_id={"ctx": peer},
        )

    def send_values(k, _):
        peer = lax.rem(me + k, lanes)
        send_v[peer] = values_of(peer)
        values_copy(me, peer).start()
        return 0

    lax.fori_loop(1, lanes, send_values, 0)
    recv_v[behind + me] = values_of(me)

    def gates(j, _):
        gate[:, aligned(j * share, share)] = conv(0, j)
        return 0

    lax.fori_loop(0, lanes, gates, 0)

    def take_values(k, _):
        peer = lax.rem(me + k, lanes)
        values_copy(peer, peer).wait_recv()
        return 0

    lax.fori_loop(1, lanes, take_values, 0)

    for g in range(own_groups):
        part = pl.ds(g * GSIZE, GSIZE)
        lhs = jnp.concatenate(
            [recv_v[b : b + lanes, part, :].reshape(lanes * GSIZE, rows) for b in range(behind + 1)],
            axis=1,
        )
        mixed = jnp.dot(lhs, toeplitz[g], preferred_element_type=jnp.float32)
        send_m[:, part, :] = mixed.astype(jnp.bfloat16).reshape(lanes, GSIZE, rows)

    def send_mixed(k, _):
        mixed_copy(me, lax.rem(me + k, lanes)).start()
        return 0

    lax.fori_loop(1, lanes, send_mixed, 0)
    recv_m[me] = send_m[me]

    def make_hidden(j):
        cols = aligned(j * share, share)
        mixed = recv_m[j].astype(jnp.float32).T
        hidden[:, cols] = (gate[:, cols] * mixed).astype(jnp.bfloat16)

    make_hidden(me)

    def take_mixed(k, _):
        peer = lax.rem(me + k, lanes)
        mixed_copy(peer, peer).wait_recv()
        make_hidden(peer)
        return 0

    lax.fori_loop(1, lanes, take_mixed, 0)
    load.wait()

    def product(device, q):
        cols = aligned((device * pieces + q) * wide, wide)
        return jnp.dot(hidden[...], held_weight[:, cols], preferred_element_type=jnp.float32)

    def core_copy(dy, q):
        return pltpu.make_async_remote_copy(
            src_ref=core_send.at[dy, q],
            dst_ref=core_recv.at[dy, q],
            send_sem=cs_sems.at[dy, q],
            recv_sem=cr_sems.at[dy, q],
            device_id={"tp": partner},
        )

    def y_copy(dy, q):
        return pltpu.make_async_remote_copy(
            src_ref=y_send.at[dy, q],
            dst_ref=y_recv.at[dy, q],
            send_sem=ys_sems.at[dy, q],
            recv_sem=yr_sems.at[dy, q],
            device_id={"tp": lax.rem(y + dy, cores_y) * 2 + core},
        )

    for dy in list(range(1, cores_y)) + [0]:
        other = lax.rem(y + dy, cores_y) * 2

        def give(q, _):
            core_send[dy, q] = product(other + 1 - core, q).astype(jnp.bfloat16)
            core_copy(dy, q).start()
            return 0

        lax.fori_loop(0, pieces, give, 0)

        def add(q, _):
            mine = product(other + core, q)
            core_copy(dy, q).wait_recv()
            mine = mine + core_recv[dy, q].astype(jnp.float32)
            if dy:
                y_send[dy, q] = mine.astype(jnp.bfloat16)
                y_copy(dy, q).start()
            else:
                for other_dy in range(1, cores_y):
                    y_copy(other_dy, q).wait_recv()
                    mine = mine + y_recv[other_dy, q].astype(jnp.float32)
                out[:, aligned(q * wide, wide)] = mine.astype(jnp.bfloat16)
            return 0

        lax.fori_loop(0, pieces, add, 0)

    def drain(k, _):
        peer = lax.rem(me + k, lanes)
        values_copy(me, peer).wait_send()
        mixed_copy(me, peer).wait_send()
        return 0

    lax.fori_loop(1, lanes, drain, 0)
    for dy in range(cores_y):

        def drain_sum(q, _):
            core_copy(dy, q).wait_send()
            if dy:
                y_copy(dy, q).wait_send()
            return 0

        lax.fori_loop(0, pieces, drain_sum, 0)


def fused(projected, short_filter, long_filter, out_weight):
    lanes, devices = lax.axis_size("ctx"), lax.axis_size("tp")
    rows, _, chans = projected.shape
    groups, reach = long_filter.shape
    features = out_weight.shape[1]
    cores_y = devices // 2
    share = chans // lanes
    behind = reach // rows
    own = features // devices
    pieces = 4
    wide = own // pieces
    bf16, f32 = jnp.bfloat16, jnp.float32
    vmem = pl.BlockSpec(memory_space=pltpu.VMEM)
    dma = pltpu.SemaphoreType.DMA
    return pl.pallas_call(
        functools.partial(fused_kernel, lanes, cores_y),
        out_shape=jax.ShapeDtypeStruct((rows, own), bf16),
        in_specs=[vmem, vmem, vmem, pl.BlockSpec(memory_space=pl.ANY)],
        out_specs=vmem,
        scratch_shapes=[
            pltpu.VMEM((chans, features), bf16),
            pltpu.VMEM((3, EDGE, chans), bf16),
            pltpu.VMEM((groups, reach + 2 * rows), f32),
            pltpu.VMEM((share // GSIZE, reach + rows, rows), bf16),
            pltpu.VMEM((rows, chans), f32),
            pltpu.VMEM((lanes, share, rows), bf16),
            pltpu.VMEM((behind + lanes, share, rows), bf16),
            pltpu.VMEM((lanes, share, rows), bf16),
            pltpu.VMEM((lanes, share, rows), bf16),
            pltpu.VMEM((rows, chans), bf16),
            pltpu.VMEM((cores_y, pieces, rows, wide), bf16),
            pltpu.VMEM((cores_y, pieces, rows, wide), bf16),
            pltpu.VMEM((cores_y, pieces, rows, wide), bf16),
            pltpu.VMEM((cores_y, pieces, rows, wide), bf16),
            dma,
            dma((2,)),
            dma((lanes,)),
            dma((lanes,)),
            dma((lanes,)),
            dma((lanes,)),
            dma((cores_y, pieces)),
            dma((cores_y, pieces)),
            dma((cores_y, pieces)),
            dma((cores_y, pieces)),
        ],
        compiler_params=pltpu.CompilerParams(
            collective_id=0, has_side_effects=True, vmem_limit_bytes=48 * 2**20
        ),
        cost_estimate=pl.CostEstimate(
            flops=2 * rows * chans * features,
            bytes_accessed=2 * chans * features,
            transcendentals=0,
        ),
    )(jnp.transpose(projected, (1, 0, 2)), short_filter, long_filter, out_weight)


def fits(projected, long_filter, out_weight):
    lanes, devices = lax.axis_size("ctx"), lax.axis_size("tp")
    rows, _, chans = projected.shape
    share = chans // lanes
    return (
        rows % 128 == 0
        and share % 128 == 0
        and share * lanes == chans
        and lanes > 1
        and devices % 2 == 0
        and long_filter.shape[1] % rows == 0
        and out_weight.shape[1] % (devices * 512) == 0
    )


def shifted(array, axis, by):
    size = lax.axis_size(axis)
    pairs = [(i, i + by) for i in range(size) if 0 <= i + by < size]
    return lax.ppermute(array, axis, pairs)


def toeplitz_block(padded_taps, lag_base, count, tok_rows):
    width = tok_rows + count - 1
    groups = padded_taps.shape[0]
    window = lax.dynamic_slice_in_dim(padded_taps, lag_base - (count - 1) + 2 * tok_rows, width, 1)
    flipped = jnp.concatenate([window[:, ::-1], jnp.zeros((groups, 1), window.dtype)], axis=1)
    tiled = jnp.tile(flipped, (1, tok_rows))
    skewed = tiled[:, : tok_rows * width].reshape(groups, tok_rows, width)
    return skewed[:, :, tok_rows - 1 : tok_rows - 1 + count]


def body(projected, short_filter, long_filter, out_weight):
    if fits(projected, long_filter, out_weight):
        return fused(projected, short_filter, long_filter, out_weight)
    tok_rows = projected.shape[0]
    taps = short_filter.shape[0]
    groups = long_filter.shape[0]
    reach = long_filter.shape[1]
    border = shifted(projected[tok_rows - (taps - 1) :], "ctx", 1)
    extended = jnp.concatenate([border, projected], axis=0).astype(jnp.float32)
    conved = short_filter[0] * extended[taps - 1 : taps - 1 + tok_rows]
    for offset in range(1, taps):
        conved = (
            conved
            + short_filter[offset] * extended[taps - 1 - offset : taps - 1 - offset + tok_rows]
        )
    values = (conved[:, 1, :] * conved[:, 2, :]).astype(jnp.bfloat16)
    padding = jnp.zeros((groups, 2 * tok_rows), long_filter.dtype)
    padded_taps = jnp.concatenate([padding, long_filter, padding], axis=1)
    lanes = lax.axis_size("ctx")
    whole = lax.all_to_all(values, "ctx", split_axis=1, concat_axis=0, tiled=True)
    share = whole.shape[1]
    held_groups = max(1, share // GSIZE)
    per_group = share // held_groups
    first_group = lax.axis_index("ctx") * share // GSIZE
    own_taps = lax.dynamic_slice_in_dim(padded_taps, first_group, held_groups, 0)
    behind = reach // tok_rows
    lead = jnp.zeros((behind * tok_rows, share), whole.dtype)
    stretched = jnp.concatenate([lead, whole], axis=0)
    blocks = stretched.reshape(behind + lanes, tok_rows, held_groups, per_group)

    def one_lag(step, total):
        matrix = toeplitz_block(own_taps, step * tok_rows, tok_rows, tok_rows)
        source = lax.dynamic_slice_in_dim(blocks, behind - step, lanes, 0)
        return total + jnp.einsum(
            "gts,osgi->otgi", matrix, source, preferred_element_type=jnp.float32
        )

    start_total = jnp.zeros((lanes, tok_rows, held_groups, per_group), jnp.float32)
    spread = lax.fori_loop(0, behind + 1, one_lag, start_total).reshape(lanes * tok_rows, share)
    mixed = lax.all_to_all(
        spread.astype(jnp.bfloat16), "ctx", split_axis=0, concat_axis=1, tiled=True
    ).astype(spread.dtype)
    hidden = (conved[:, 0, :] * mixed).astype(jnp.bfloat16)
    partial_sum = jnp.dot(hidden, out_weight, preferred_element_type=jnp.float32)
    return lax.psum_scatter(partial_sum.astype(jnp.bfloat16), "tp", scatter_dimension=1, tiled=True)


def solution(mesh):
    return jax.shard_map(
        body,
        mesh=mesh,
        in_specs=(P("ctx", None, "tp"), P(None, None, "tp"), P("tp", None), P("tp", None)),
        out_specs=P("ctx", "tp"),
        check_vma=False,
    )
```

```python
import functools

import jax
import jax.numpy as jnp
from jax import lax
from jax.experimental import pallas as pl
from jax.experimental.pallas import tpu as pltpu
from jax.sharding import PartitionSpec as P

GSIZE = 16
EDGE = 16


def aligned(start, size):
    return pl.ds(pl.multiple_of(start, size), size)


def fused_kernel(
    lanes,
    cores_y,
    proj_hbm,
    short_hbm,
    longf_hbm,
    weight,
    out,
    proj,
    short,
    longf,
    held_weight,
    border,
    padded,
    toeplitz,
    gate,
    values,
    send_v,
    recv_v,
    send_m,
    recv_m,
    hidden,
    core_send,
    core_recv,
    y_send,
    y_recv,
    load_sems,
    edge_sem,
    v_sems,
    v_recvs,
    m_sems,
    m_recvs,
    cs_sems,
    cr_sems,
    ys_sems,
    yr_sems,
):
    me = lax.axis_index("ctx")
    tp = lax.axis_index("tp")
    y, core = tp // 2, tp % 2
    partner = y * 2 + (1 - core)
    _, rows, chans = proj.shape
    taps = short.shape[1]
    reach = longf.shape[1]
    behind = reach // rows
    share = chans // lanes
    own_groups = share // GSIZE
    pieces, wide = y_send.shape[1], y_send.shape[3]

    loads = [
        pltpu.make_async_copy(source, target, load_sems.at[i])
        for i, (source, target) in enumerate(
            [(longf_hbm, longf), (proj_hbm, proj), (short_hbm, short), (weight, held_weight)]
        )
    ]
    for load in loads:
        load.start()

    barrier = pltpu.get_barrier_semaphore()
    for k in range(1, lanes):
        pl.semaphore_signal(barrier, inc=1, device_id={"ctx": lax.rem(me + k, lanes)})
    pl.semaphore_signal(barrier, inc=1, device_id={"tp": partner})
    for dy in range(1, cores_y):
        pl.semaphore_signal(
            barrier, inc=1, device_id={"tp": lax.rem(y + dy, cores_y) * 2 + core}
        )
    loads[0].wait()
    groups = longf.shape[0]
    padded[:, 0:rows] = jnp.zeros((groups, rows), jnp.float32)
    padded[:, rows : rows + reach] = longf[...].astype(jnp.float32)
    padded[:, rows + reach :] = jnp.zeros((groups, rows), jnp.float32)
    recv_v[0:behind] = jnp.zeros((behind, share, rows), jnp.bfloat16)

    def build(g, _):
        line = padded[pl.ds(me * own_groups + g, 1), :]
        flat = jnp.broadcast_to(line, (rows, reach + 2 * rows))
        skewed = pltpu.roll(flat, 0, 1, stride=1, stride_axis=0)
        for b in range(behind + 1):
            low = rows + reach - rows * b
            toeplitz[g, b * rows : (b + 1) * rows, :] = skewed[:, low : low + rows].astype(jnp.bfloat16)
        return 0

    lax.fori_loop(0, own_groups, build, 0)
    pl.semaphore_wait(barrier, lanes - 1 + 1 + cores_y - 1)

    edge = pltpu.make_async_remote_copy(
        src_ref=proj_hbm.at[:, pl.ds(rows - EDGE, EDGE), :],
        dst_ref=border,
        send_sem=edge_sem.at[0],
        recv_sem=edge_sem.at[1],
        device_id={"ctx": lax.rem(me + 1, lanes)},
    )
    edge.start()


    loads[1].wait()
    loads[2].wait()

    def taps_over(ext, p, cols):
        total = short[p, 0:1, cols] * ext[EDGE:]
        for d in range(1, taps):
            total = total + short[p, d : d + 1, cols] * pltpu.roll(ext, d, 0)[EDGE:]
        return total

    def inner(p, j):
        return taps_over(proj[p, :, aligned(j * share, share)].astype(jnp.float32), p, aligned(j * share, share))

    def outer(p, j):
        cols = aligned(j * share, share)
        before = jnp.where(me == 0, 0.0, border[p, :, cols].astype(jnp.float32))
        first = proj[p, 0:EDGE, cols].astype(jnp.float32)
        return taps_over(jnp.concatenate([before, first], axis=0), p, cols)

    def inner_rows(j, _):
        cols = aligned(j * share, share)
        values[EDGE:, cols] = inner(1, j) * inner(2, j)
        gate[EDGE:, cols] = inner(0, j)
        return 0

    lax.fori_loop(0, lanes, inner_rows, 0)
    edge.wait()

    def values_of(j):
        cols = aligned(j * share, share)
        values[0:EDGE, cols] = outer(1, j) * outer(2, j)
        return values[:, cols].T.astype(jnp.bfloat16)

    def values_copy(slot, peer):
        return pltpu.make_async_remote_copy(
            src_ref=send_v.at[peer],
            dst_ref=recv_v.at[behind + slot],
            send_sem=v_sems.at[peer],
            recv_sem=v_recvs.at[slot],
            device_id={"ctx": peer},
        )

    half = share // 2

    def mixed_copy(slot, peer, h):
        part = pl.ds(h * half, half)
        return pltpu.make_async_remote_copy(
            src_ref=send_m.at[peer, part],
            dst_ref=recv_m.at[slot, part],
            send_sem=m_sems.at[h, peer],
            recv_sem=m_recvs.at[h, slot],
            device_id={"ctx": peer},
        )

    def send_values(k, _):
        peer = lax.rem(me + k, lanes)
        send_v[peer] = values_of(peer)
        values_copy(me, peer).start()
        return 0

    lax.fori_loop(1, lanes, send_values, 0)
    recv_v[behind + me] = values_of(me)

    def gates(j, _):
        gate[0:EDGE, aligned(j * share, share)] = outer(0, j)
        return 0

    lax.fori_loop(0, lanes, gates, 0)

    def take_values(k, _):
        peer = lax.rem(me + k, lanes)
        values_copy(peer, peer).wait_recv()
        return 0

    lax.fori_loop(1, lanes, take_values, 0)

    def send_mixed(h):
        def start(k, _):
            mixed_copy(me, lax.rem(me + k, lanes), h).start()
            return 0

        lax.fori_loop(1, lanes, start, 0)

    for g in range(own_groups):
        part = pl.ds(g * GSIZE, GSIZE)
        lhs = jnp.concatenate(
            [recv_v[b : b + lanes, part, :].reshape(lanes * GSIZE, rows) for b in range(behind + 1)],
            axis=1,
        )
        mixed = jnp.dot(lhs, toeplitz[g], preferred_element_type=jnp.float32)
        send_m[:, part, :] = mixed.astype(jnp.bfloat16).reshape(lanes, GSIZE, rows)
        if (g + 1) * GSIZE % half == 0:
            send_mixed(((g + 1) * GSIZE - 1) // half)

    recv_m[me] = send_m[me]

    def make_hidden(j):
        cols = aligned(j * share, share)
        mixed = recv_m[j].astype(jnp.float32).T
        hidden[:, cols] = (gate[:, cols] * mixed).astype(jnp.bfloat16)

    make_hidden(me)

    def take_mixed(k, _):
        peer = lax.rem(me + k, lanes)
        mixed_copy(peer, peer, 0).wait_recv()
        mixed_copy(peer, peer, 1).wait_recv()
        make_hidden(peer)
        return 0

    lax.fori_loop(1, lanes, take_mixed, 0)
    loads[3].wait()

    def product(device, q):
        cols = aligned((device * pieces + q) * wide, wide)
        return jnp.dot(hidden[...], held_weight[:, cols], preferred_element_type=jnp.float32)

    def core_copy(dy, q):
        return pltpu.make_async_remote_copy(
            src_ref=core_send.at[dy, q],
            dst_ref=core_recv.at[dy, q],
            send_sem=cs_sems.at[dy, q],
            recv_sem=cr_sems.at[dy, q],
            device_id={"tp": partner},
        )

    def y_copy(dy, q):
        return pltpu.make_async_remote_copy(
            src_ref=y_send.at[dy, q],
            dst_ref=y_recv.at[dy, q],
            send_sem=ys_sems.at[dy, q],
            recv_sem=yr_sems.at[dy, q],
            device_id={"tp": lax.rem(y + dy, cores_y) * 2 + core},
        )

    for dy in list(range(1, cores_y)) + [0]:
        other = lax.rem(y + dy, cores_y) * 2

        def give(q, _):
            core_send[dy, q] = product(other + 1 - core, q).astype(jnp.bfloat16)
            core_copy(dy, q).start()
            return 0

        def add(q, _):
            mine = product(other + core, q)
            core_copy(dy, q).wait_recv()
            mine = mine + core_recv[dy, q].astype(jnp.float32)
            if dy:
                y_send[dy, q] = mine.astype(jnp.bfloat16)
                y_copy(dy, q).start()
            else:
                for other_dy in range(1, cores_y):
                    y_copy(other_dy, q).wait_recv()
                    mine = mine + y_recv[other_dy, q].astype(jnp.float32)
                out[:, aligned(q * wide, wide)] = mine.astype(jnp.bfloat16)
            return 0

        def both(q, _):
            give(q + 1, 0)
            return add(q, 0)

        if dy:
            give(0, 0)
            lax.fori_loop(0, pieces - 1, both, 0)
            add(pieces - 1, 0)
        else:
            lax.fori_loop(0, pieces, give, 0)
            lax.fori_loop(0, pieces, add, 0)

    def drain(k, _):
        peer = lax.rem(me + k, lanes)
        values_copy(me, peer).wait_send()
        mixed_copy(me, peer, 0).wait_send()
        mixed_copy(me, peer, 1).wait_send()
        return 0

    lax.fori_loop(1, lanes, drain, 0)
    for dy in range(cores_y):

        def drain_sum(q, _):
            core_copy(dy, q).wait_send()
            if dy:
                y_copy(dy, q).wait_send()
            return 0

        lax.fori_loop(0, pieces, drain_sum, 0)


def fused(projected, short_filter, long_filter, out_weight):
    lanes, devices = lax.axis_size("ctx"), lax.axis_size("tp")
    rows, _, chans = projected.shape
    groups, reach = long_filter.shape
    features = out_weight.shape[1]
    cores_y = devices // 2
    share = chans // lanes
    behind = reach // rows
    own = features // devices
    pieces = 4
    wide = own // pieces
    bf16, f32 = jnp.bfloat16, jnp.float32
    vmem = pl.BlockSpec(memory_space=pltpu.VMEM)
    hbm = pl.BlockSpec(memory_space=pltpu.HBM)
    taps = short_filter.shape[0]
    dma = pltpu.SemaphoreType.DMA
    return pl.pallas_call(
        functools.partial(fused_kernel, lanes, cores_y),
        out_shape=jax.ShapeDtypeStruct((rows, own), bf16),
        in_specs=[hbm] * 4,
        out_specs=vmem,
        scratch_shapes=[
            pltpu.VMEM((3, rows, chans), bf16),
            pltpu.VMEM((3, taps, chans), f32),
            pltpu.VMEM((groups, reach), bf16),
            pltpu.VMEM((chans, features), bf16),
            pltpu.VMEM((3, EDGE, chans), bf16),
            pltpu.VMEM((groups, reach + 2 * rows), f32),
            pltpu.VMEM((share // GSIZE, reach + rows, rows), bf16),
            pltpu.VMEM((rows, chans), f32),
            pltpu.VMEM((rows, chans), f32),
            pltpu.VMEM((lanes, share, rows), bf16),
            pltpu.VMEM((behind + lanes, share, rows), bf16),
            pltpu.VMEM((lanes, share, rows), bf16),
            pltpu.VMEM((lanes, share, rows), bf16),
            pltpu.VMEM((rows, chans), bf16),
            pltpu.VMEM((cores_y, pieces, rows, wide), bf16),
            pltpu.VMEM((cores_y, pieces, rows, wide), bf16),
            pltpu.VMEM((cores_y, pieces, rows, wide), bf16),
            pltpu.VMEM((cores_y, pieces, rows, wide), bf16),
            dma((4,)),
            dma((2,)),
            dma((lanes,)),
            dma((lanes,)),
            dma((2, lanes)),
            dma((2, lanes)),
            dma((cores_y, pieces)),
            dma((cores_y, pieces)),
            dma((cores_y, pieces)),
            dma((cores_y, pieces)),
        ],
        compiler_params=pltpu.CompilerParams(
            collective_id=0, has_side_effects=True, vmem_limit_bytes=62 * 2**20
        ),
        cost_estimate=pl.CostEstimate(
            flops=2 * rows * chans * features,
            bytes_accessed=2 * chans * features,
            transcendentals=0,
        ),
    )(jnp.transpose(projected, (1, 0, 2)), jnp.transpose(short_filter, (1, 0, 2)), long_filter, out_weight)


def fits(projected, long_filter, out_weight):
    lanes, devices = lax.axis_size("ctx"), lax.axis_size("tp")
    rows, _, chans = projected.shape
    share = chans // lanes
    return (
        rows % 128 == 0
        and share % 128 == 0
        and share * lanes == chans
        and lanes > 1
        and devices % 2 == 0
        and long_filter.shape[1] % rows == 0
        and out_weight.shape[1] % (devices * 512) == 0
    )


def shifted(array, axis, by):
    size = lax.axis_size(axis)
    pairs = [(i, i + by) for i in range(size) if 0 <= i + by < size]
    return lax.ppermute(array, axis, pairs)


def toeplitz_block(padded_taps, lag_base, count, tok_rows):
    width = tok_rows + count - 1
    groups = padded_taps.shape[0]
    window = lax.dynamic_slice_in_dim(padded_taps, lag_base - (count - 1) + 2 * tok_rows, width, 1)
    flipped = jnp.concatenate([window[:, ::-1], jnp.zeros((groups, 1), window.dtype)], axis=1)
    tiled = jnp.tile(flipped, (1, tok_rows))
    skewed = tiled[:, : tok_rows * width].reshape(groups, tok_rows, width)
    return skewed[:, :, tok_rows - 1 : tok_rows - 1 + count]


def body(projected, short_filter, long_filter, out_weight):
    if fits(projected, long_filter, out_weight):
        return fused(projected, short_filter, long_filter, out_weight)
    tok_rows = projected.shape[0]
    taps = short_filter.shape[0]
    groups = long_filter.shape[0]
    reach = long_filter.shape[1]
    border = shifted(projected[tok_rows - (taps - 1) :], "ctx", 1)
    extended = jnp.concatenate([border, projected], axis=0).astype(jnp.float32)
    conved = short_filter[0] * extended[taps - 1 : taps - 1 + tok_rows]
    for offset in range(1, taps):
        conved = (
            conved
            + short_filter[offset] * extended[taps - 1 - offset : taps - 1 - offset + tok_rows]
        )
    values = (conved[:, 1, :] * conved[:, 2, :]).astype(jnp.bfloat16)
    padding = jnp.zeros((groups, 2 * tok_rows), long_filter.dtype)
    padded_taps = jnp.concatenate([padding, long_filter, padding], axis=1)
    lanes = lax.axis_size("ctx")
    whole = lax.all_to_all(values, "ctx", split_axis=1, concat_axis=0, tiled=True)
    share = whole.shape[1]
    held_groups = max(1, share // GSIZE)
    per_group = share // held_groups
    first_group = lax.axis_index("ctx") * share // GSIZE
    own_taps = lax.dynamic_slice_in_dim(padded_taps, first_group, held_groups, 0)
    behind = reach // tok_rows
    lead = jnp.zeros((behind * tok_rows, share), whole.dtype)
    stretched = jnp.concatenate([lead, whole], axis=0)
    blocks = stretched.reshape(behind + lanes, tok_rows, held_groups, per_group)

    def one_lag(step, total):
        matrix = toeplitz_block(own_taps, step * tok_rows, tok_rows, tok_rows)
        source = lax.dynamic_slice_in_dim(blocks, behind - step, lanes, 0)
        return total + jnp.einsum(
            "gts,osgi->otgi", matrix, source, preferred_element_type=jnp.float32
        )

    start_total = jnp.zeros((lanes, tok_rows, held_groups, per_group), jnp.float32)
    spread = lax.fori_loop(0, behind + 1, one_lag, start_total).reshape(lanes * tok_rows, share)
    mixed = lax.all_to_all(
        spread.astype(jnp.bfloat16), "ctx", split_axis=0, concat_axis=1, tiled=True
    ).astype(spread.dtype)
    hidden = (conved[:, 0, :] * mixed).astype(jnp.bfloat16)
    partial_sum = jnp.dot(hidden, out_weight, preferred_element_type=jnp.float32)
    return lax.psum_scatter(partial_sum.astype(jnp.bfloat16), "tp", scatter_dimension=1, tiled=True)


def solution(mesh):
    return jax.shard_map(
        body,
        mesh=mesh,
        in_specs=(P("ctx", None, "tp"), P(None, None, "tp"), P("tp", None), P("tp", None)),
        out_specs=P("ctx", "tp"),
        check_vma=False,
    )
```

```python
import functools

import jax
import jax.numpy as jnp
from jax import lax
from jax.experimental import pallas as pl
from jax.experimental.pallas import tpu as pltpu
from jax.sharding import PartitionSpec as P

GSIZE = 16
EDGE = 16


def aligned(start, size):
    return pl.ds(pl.multiple_of(start, size), size)


def fused_kernel(
    lanes,
    cores_y,
    proj_hbm,
    short_hbm,
    longf_hbm,
    weight,
    out,
    proj,
    short,
    longf,
    held_weight,
    border,
    padded,
    toeplitz,
    gate,
    values,
    send_v,
    recv_v,
    send_m,
    recv_m,
    hidden,
    core_send,
    core_recv,
    y_send,
    y_recv,
    load_sems,
    edge_sem,
    v_sems,
    v_recvs,
    m_sems,
    m_recvs,
    cs_sems,
    cr_sems,
    ys_sems,
    yr_sems,
):
    me = lax.axis_index("ctx")
    tp = lax.axis_index("tp")
    y, core = tp // 2, tp % 2
    partner = y * 2 + (1 - core)
    _, rows, chans = proj.shape
    taps = short.shape[1]
    reach = longf.shape[1]
    behind = reach // rows
    share = chans // lanes
    own_groups = share // GSIZE
    pieces, wide = y_send.shape[1], y_send.shape[3]

    loads = [
        pltpu.make_async_copy(source, target, load_sems.at[i])
        for i, (source, target) in enumerate(
            [(longf_hbm, longf), (proj_hbm, proj), (short_hbm, short), (weight, held_weight)]
        )
    ]
    for load in loads:
        load.start()

    barrier = pltpu.get_barrier_semaphore()
    for k in range(1, lanes):
        pl.semaphore_signal(barrier, inc=1, device_id={"ctx": lax.rem(me + k, lanes)})
    pl.semaphore_signal(barrier, inc=1, device_id={"tp": partner})
    for dy in range(1, cores_y):
        pl.semaphore_signal(
            barrier, inc=1, device_id={"tp": lax.rem(y + dy, cores_y) * 2 + core}
        )
    loads[0].wait()
    groups = longf.shape[0]
    padded[:, 0:rows] = jnp.zeros((groups, rows), jnp.float32)
    padded[:, rows : rows + reach] = longf[...].astype(jnp.float32)
    padded[:, rows + reach :] = jnp.zeros((groups, rows), jnp.float32)
    recv_v[0:behind] = jnp.zeros((behind, share, rows), jnp.bfloat16)

    def build(g, _):
        line = padded[pl.ds(me * own_groups + g, 1), :]
        flat = jnp.broadcast_to(line, (rows, reach + 2 * rows))
        skewed = pltpu.roll(flat, 0, 1, stride=1, stride_axis=0)
        for b in range(behind + 1):
            low = rows + reach - rows * b
            toeplitz[g, b * rows : (b + 1) * rows, :] = skewed[:, low : low + rows].astype(jnp.bfloat16)
        return 0

    lax.fori_loop(0, own_groups, build, 0)
    pl.semaphore_wait(barrier, lanes - 1 + 1 + cores_y - 1)

    edge = pltpu.make_async_remote_copy(
        src_ref=proj_hbm.at[:, pl.ds(rows - EDGE, EDGE), :],
        dst_ref=border,
        send_sem=edge_sem.at[0],
        recv_sem=edge_sem.at[1],
        device_id={"ctx": lax.rem(me + 1, lanes)},
    )
    edge.start()


    loads[1].wait()
    loads[2].wait()

    def taps_over(ext, p, cols):
        total = short[p, 0:1, cols] * ext[EDGE:]
        for d in range(1, taps):
            total = total + short[p, d : d + 1, cols] * pltpu.roll(ext, d, 0)[EDGE:]
        return total

    def inner(p, j):
        return taps_over(proj[p, :, aligned(j * share, share)].astype(jnp.float32), p, aligned(j * share, share))

    def outer(p, j):
        cols = aligned(j * share, share)
        before = jnp.where(me == 0, 0.0, border[p, :, cols].astype(jnp.float32))
        first = proj[p, 0:EDGE, cols].astype(jnp.float32)
        return taps_over(jnp.concatenate([before, first], axis=0), p, cols)

    def inner_rows(j, _):
        cols = aligned(j * share, share)
        values[EDGE:, cols] = inner(1, j) * inner(2, j)
        gate[EDGE:, cols] = inner(0, j)
        return 0

    lax.fori_loop(0, lanes, inner_rows, 0)
    edge.wait()

    def values_of(j):
        cols = aligned(j * share, share)
        values[0:EDGE, cols] = outer(1, j) * outer(2, j)
        return values[:, cols].T.astype(jnp.bfloat16)

    def values_copy(slot, peer):
        return pltpu.make_async_remote_copy(
            src_ref=send_v.at[peer],
            dst_ref=recv_v.at[behind + slot],
            send_sem=v_sems.at[peer],
            recv_sem=v_recvs.at[slot],
            device_id={"ctx": peer},
        )

    half = share // 2

    def far_first(i):
        k = lanes // 2 + (i + 1) // 2 * (2 * (i % 2) - 1)
        return lax.rem(me + k, lanes)

    def mixed_copy(slot, peer, h):
        part = pl.ds(h * half, half)
        return pltpu.make_async_remote_copy(
            src_ref=send_m.at[peer, part],
            dst_ref=recv_m.at[slot, part],
            send_sem=m_sems.at[h, peer],
            recv_sem=m_recvs.at[h, slot],
            device_id={"ctx": peer},
        )

    def send_values(i, _):
        peer = far_first(i)
        send_v[peer] = values_of(peer)
        values_copy(me, peer).start()
        return 0

    lax.fori_loop(0, lanes - 1, send_values, 0)
    recv_v[behind + me] = values_of(me)

    def gates(j, _):
        gate[0:EDGE, aligned(j * share, share)] = outer(0, j)
        return 0

    lax.fori_loop(0, lanes, gates, 0)

    def take_values(i, _):
        peer = far_first(i)
        values_copy(peer, peer).wait_recv()
        return 0

    lax.fori_loop(0, lanes - 1, take_values, 0)

    def send_mixed(h):
        def start(i, _):
            mixed_copy(me, far_first(i), h).start()
            return 0

        lax.fori_loop(0, lanes - 1, start, 0)

    for g in range(own_groups):
        part = pl.ds(g * GSIZE, GSIZE)
        lhs = jnp.concatenate(
            [recv_v[b : b + lanes, part, :].reshape(lanes * GSIZE, rows) for b in range(behind + 1)],
            axis=1,
        )
        mixed = jnp.dot(lhs, toeplitz[g], preferred_element_type=jnp.float32)
        send_m[:, part, :] = mixed.astype(jnp.bfloat16).reshape(lanes, GSIZE, rows)
        if (g + 1) * GSIZE % half == 0:
            send_mixed(((g + 1) * GSIZE - 1) // half)

    recv_m[me] = send_m[me]

    def make_hidden(j):
        cols = aligned(j * share, share)
        mixed = recv_m[j].astype(jnp.float32).T
        hidden[:, cols] = (gate[:, cols] * mixed).astype(jnp.bfloat16)

    make_hidden(me)

    def take_mixed(i, _):
        peer = far_first(i)
        mixed_copy(peer, peer, 0).wait_recv()
        mixed_copy(peer, peer, 1).wait_recv()
        make_hidden(peer)
        return 0

    lax.fori_loop(0, lanes - 1, take_mixed, 0)
    loads[3].wait()

    def product(device, q):
        cols = aligned((device * pieces + q) * wide, wide)
        return jnp.dot(hidden[...], held_weight[:, cols], preferred_element_type=jnp.float32)

    def core_copy(dy, q):
        return pltpu.make_async_remote_copy(
            src_ref=core_send.at[dy, q],
            dst_ref=core_recv.at[dy, q],
            send_sem=cs_sems.at[dy, q],
            recv_sem=cr_sems.at[dy, q],
            device_id={"tp": partner},
        )

    def y_copy(dy, q):
        return pltpu.make_async_remote_copy(
            src_ref=y_send.at[dy, q],
            dst_ref=y_recv.at[dy, q],
            send_sem=ys_sems.at[dy, q],
            recv_sem=yr_sems.at[dy, q],
            device_id={"tp": lax.rem(y + dy, cores_y) * 2 + core},
        )

    for dy in list(range(1, cores_y)) + [0]:
        other = lax.rem(y + dy, cores_y) * 2

        def give(q, _):
            core_send[dy, q] = product(other + 1 - core, q).astype(jnp.bfloat16)
            core_copy(dy, q).start()
            return 0

        def add(q, _):
            mine = product(other + core, q)
            core_copy(dy, q).wait_recv()
            mine = mine + core_recv[dy, q].astype(jnp.float32)
            if dy:
                y_send[dy, q] = mine.astype(jnp.bfloat16)
                y_copy(dy, q).start()
            else:
                for other_dy in range(1, cores_y):
                    y_copy(other_dy, q).wait_recv()
                    mine = mine + y_recv[other_dy, q].astype(jnp.float32)
                out[:, aligned(q * wide, wide)] = mine.astype(jnp.bfloat16)
            return 0

        def both(q, _):
            give(q + 1, 0)
            return add(q, 0)

        if dy:
            give(0, 0)
            lax.fori_loop(0, pieces - 1, both, 0)
            add(pieces - 1, 0)
        else:
            lax.fori_loop(0, pieces, give, 0)
            lax.fori_loop(0, pieces, add, 0)

    def drain(k, _):
        peer = lax.rem(me + k, lanes)
        values_copy(me, peer).wait_send()
        mixed_copy(me, peer, 0).wait_send()
        mixed_copy(me, peer, 1).wait_send()
        return 0

    lax.fori_loop(1, lanes, drain, 0)
    for dy in range(cores_y):

        def drain_sum(q, _):
            core_copy(dy, q).wait_send()
            if dy:
                y_copy(dy, q).wait_send()
            return 0

        lax.fori_loop(0, pieces, drain_sum, 0)


def fused(projected, short_filter, long_filter, out_weight):
    lanes, devices = lax.axis_size("ctx"), lax.axis_size("tp")
    rows, _, chans = projected.shape
    groups, reach = long_filter.shape
    features = out_weight.shape[1]
    cores_y = devices // 2
    share = chans // lanes
    behind = reach // rows
    own = features // devices
    pieces = 8
    wide = own // pieces
    bf16, f32 = jnp.bfloat16, jnp.float32
    vmem = pl.BlockSpec(memory_space=pltpu.VMEM)
    hbm = pl.BlockSpec(memory_space=pltpu.HBM)
    taps = short_filter.shape[0]
    dma = pltpu.SemaphoreType.DMA
    return pl.pallas_call(
        functools.partial(fused_kernel, lanes, cores_y),
        out_shape=pltpu.VMEM((rows, own), bf16),
        in_specs=[hbm] * 4,
        out_specs=vmem,
        scratch_shapes=[
            pltpu.VMEM((3, rows, chans), bf16),
            pltpu.VMEM((3, taps, chans), f32),
            pltpu.VMEM((groups, reach), bf16),
            pltpu.VMEM((chans, features), bf16),
            pltpu.VMEM((3, EDGE, chans), bf16),
            pltpu.VMEM((groups, reach + 2 * rows), f32),
            pltpu.VMEM((share // GSIZE, reach + rows, rows), bf16),
            pltpu.VMEM((rows, chans), f32),
            pltpu.VMEM((rows, chans), f32),
            pltpu.VMEM((lanes, share, rows), bf16),
            pltpu.VMEM((behind + lanes, share, rows), bf16),
            pltpu.VMEM((lanes, share, rows), bf16),
            pltpu.VMEM((lanes, share, rows), bf16),
            pltpu.VMEM((rows, chans), bf16),
            pltpu.VMEM((cores_y, pieces, rows, wide), bf16),
            pltpu.VMEM((cores_y, pieces, rows, wide), bf16),
            pltpu.VMEM((cores_y, pieces, rows, wide), bf16),
            pltpu.VMEM((cores_y, pieces, rows, wide), bf16),
            dma((4,)),
            dma((2,)),
            dma((lanes,)),
            dma((lanes,)),
            dma((2, lanes)),
            dma((2, lanes)),
            dma((cores_y, pieces)),
            dma((cores_y, pieces)),
            dma((cores_y, pieces)),
            dma((cores_y, pieces)),
        ],
        compiler_params=pltpu.CompilerParams(
            collective_id=0, has_side_effects=True, vmem_limit_bytes=62 * 2**20
        ),
        cost_estimate=pl.CostEstimate(
            flops=2 * rows * chans * features,
            bytes_accessed=2 * chans * features,
            transcendentals=0,
        ),
    )(jnp.transpose(projected, (1, 0, 2)), jnp.transpose(short_filter, (1, 0, 2)), long_filter, out_weight)


def fits(projected, long_filter, out_weight):
    lanes, devices = lax.axis_size("ctx"), lax.axis_size("tp")
    rows, _, chans = projected.shape
    share = chans // lanes
    return (
        rows % 128 == 0
        and share % 128 == 0
        and share * lanes == chans
        and lanes % 2 == 0
        and devices % 2 == 0
        and long_filter.shape[1] % rows == 0
        and out_weight.shape[1] % (devices * 1024) == 0
    )


def shifted(array, axis, by):
    size = lax.axis_size(axis)
    pairs = [(i, i + by) for i in range(size) if 0 <= i + by < size]
    return lax.ppermute(array, axis, pairs)


def toeplitz_block(padded_taps, lag_base, count, tok_rows):
    width = tok_rows + count - 1
    groups = padded_taps.shape[0]
    window = lax.dynamic_slice_in_dim(padded_taps, lag_base - (count - 1) + 2 * tok_rows, width, 1)
    flipped = jnp.concatenate([window[:, ::-1], jnp.zeros((groups, 1), window.dtype)], axis=1)
    tiled = jnp.tile(flipped, (1, tok_rows))
    skewed = tiled[:, : tok_rows * width].reshape(groups, tok_rows, width)
    return skewed[:, :, tok_rows - 1 : tok_rows - 1 + count]


def body(projected, short_filter, long_filter, out_weight):
    if fits(projected, long_filter, out_weight):
        return fused(projected, short_filter, long_filter, out_weight)
    tok_rows = projected.shape[0]
    taps = short_filter.shape[0]
    groups = long_filter.shape[0]
    reach = long_filter.shape[1]
    border = shifted(projected[tok_rows - (taps - 1) :], "ctx", 1)
    extended = jnp.concatenate([border, projected], axis=0).astype(jnp.float32)
    conved = short_filter[0] * extended[taps - 1 : taps - 1 + tok_rows]
    for offset in range(1, taps):
        conved = (
            conved
            + short_filter[offset] * extended[taps - 1 - offset : taps - 1 - offset + tok_rows]
        )
    values = (conved[:, 1, :] * conved[:, 2, :]).astype(jnp.bfloat16)
    padding = jnp.zeros((groups, 2 * tok_rows), long_filter.dtype)
    padded_taps = jnp.concatenate([padding, long_filter, padding], axis=1)
    lanes = lax.axis_size("ctx")
    whole = lax.all_to_all(values, "ctx", split_axis=1, concat_axis=0, tiled=True)
    share = whole.shape[1]
    held_groups = max(1, share // GSIZE)
    per_group = share // held_groups
    first_group = lax.axis_index("ctx") * share // GSIZE
    own_taps = lax.dynamic_slice_in_dim(padded_taps, first_group, held_groups, 0)
    behind = reach // tok_rows
    lead = jnp.zeros((behind * tok_rows, share), whole.dtype)
    stretched = jnp.concatenate([lead, whole], axis=0)
    blocks = stretched.reshape(behind + lanes, tok_rows, held_groups, per_group)

    def one_lag(step, total):
        matrix = toeplitz_block(own_taps, step * tok_rows, tok_rows, tok_rows)
        source = lax.dynamic_slice_in_dim(blocks, behind - step, lanes, 0)
        return total + jnp.einsum(
            "gts,osgi->otgi", matrix, source, preferred_element_type=jnp.float32
        )

    start_total = jnp.zeros((lanes, tok_rows, held_groups, per_group), jnp.float32)
    spread = lax.fori_loop(0, behind + 1, one_lag, start_total).reshape(lanes * tok_rows, share)
    mixed = lax.all_to_all(
        spread.astype(jnp.bfloat16), "ctx", split_axis=0, concat_axis=1, tiled=True
    ).astype(spread.dtype)
    hidden = (conved[:, 0, :] * mixed).astype(jnp.bfloat16)
    partial_sum = jnp.dot(hidden, out_weight, preferred_element_type=jnp.float32)
    return lax.psum_scatter(partial_sum.astype(jnp.bfloat16), "tp", scatter_dimension=1, tiled=True)


def solution(mesh):
    return jax.shard_map(
        body,
        mesh=mesh,
        in_specs=(P("ctx", None, "tp"), P(None, None, "tp"), P("tp", None), P("tp", None)),
        out_specs=P("ctx", "tp"),
        check_vma=False,
    )
```

```python
import functools

import jax
import jax.numpy as jnp
from jax import lax
from jax.experimental import pallas as pl
from jax.experimental.pallas import tpu as pltpu
from jax.sharding import PartitionSpec as P

GSIZE = 16
EDGE = 16


def aligned(start, size):
    return pl.ds(pl.multiple_of(start, size), size)


def fused_kernel(
    lanes,
    cores_y,
    proj_hbm,
    short_hbm,
    longf_hbm,
    weight,
    out,
    proj,
    short,
    longf,
    held_weight,
    border,
    padded,
    toeplitz,
    gate,
    values,
    send_v,
    recv_v,
    send_m,
    recv_m,
    hidden,
    core_send,
    core_recv,
    y_send,
    y_recv,
    load_sems,
    edge_sem,
    v_sems,
    v_recvs,
    m_sems,
    m_recvs,
    cs_sems,
    cr_sems,
    ys_sems,
    yr_sems,
):
    me = lax.axis_index("ctx")
    tp = lax.axis_index("tp")
    y, core = tp // 2, tp % 2
    partner = y * 2 + (1 - core)
    _, rows, chans = proj.shape
    taps = short.shape[1]
    reach = longf.shape[1]
    behind = reach // rows
    share = chans // lanes
    own_groups = share // GSIZE
    pieces, wide = y_send.shape[1], y_send.shape[3]

    loads = [
        pltpu.make_async_copy(source, target, load_sems.at[i])
        for i, (source, target) in enumerate(
            [(longf_hbm, longf), (proj_hbm, proj), (short_hbm, short), (weight, held_weight)]
        )
    ]
    for load in loads:
        load.start()

    barrier = pltpu.get_barrier_semaphore()
    for k in range(1, lanes):
        pl.semaphore_signal(barrier, inc=1, device_id={"ctx": lax.rem(me + k, lanes)})
    pl.semaphore_signal(barrier, inc=1, device_id={"tp": partner})
    for dy in range(1, cores_y):
        pl.semaphore_signal(
            barrier, inc=1, device_id={"tp": lax.rem(y + dy, cores_y) * 2 + core}
        )
    pl.semaphore_wait(barrier, lanes - 1 + 1 + cores_y - 1)

    edge = pltpu.make_async_remote_copy(
        src_ref=proj_hbm.at[:, pl.ds(rows - EDGE, EDGE), :],
        dst_ref=border,
        send_sem=edge_sem.at[0],
        recv_sem=edge_sem.at[1],
        device_id={"ctx": lax.rem(me + 1, lanes)},
    )
    edge.start()
    loads[0].wait()
    groups = longf.shape[0]
    padded[:, 0:rows] = jnp.zeros((groups, rows), jnp.float32)
    padded[:, rows : rows + reach] = longf[...].astype(jnp.float32)
    padded[:, rows + reach :] = jnp.zeros((groups, rows), jnp.float32)
    recv_v[0:behind] = jnp.zeros((behind, share, rows), jnp.bfloat16)

    def build(g, _):
        line = padded[pl.ds(me * own_groups + g, 1), :]
        flat = jnp.broadcast_to(line, (rows, reach + 2 * rows))
        skewed = pltpu.roll(flat, 0, 1, stride=1, stride_axis=0)
        for b in range(behind + 1):
            low = rows + reach - rows * b
            toeplitz[g, b * rows : (b + 1) * rows, :] = skewed[:, low : low + rows].astype(jnp.bfloat16)
        return 0

    lax.fori_loop(0, own_groups, build, 0)


    loads[1].wait()
    loads[2].wait()

    def taps_over(ext, p, cols):
        total = short[p, 0:1, cols] * ext[EDGE:]
        for d in range(1, taps):
            total = total + short[p, d : d + 1, cols] * pltpu.roll(ext, d, 0)[EDGE:]
        return total

    def inner(p, j):
        return taps_over(proj[p, :, aligned(j * share, share)].astype(jnp.float32), p, aligned(j * share, share))

    def outer(p, j):
        cols = aligned(j * share, share)
        before = jnp.where(me == 0, 0.0, border[p, :, cols].astype(jnp.float32))
        first = proj[p, 0:EDGE, cols].astype(jnp.float32)
        return taps_over(jnp.concatenate([before, first], axis=0), p, cols)

    def inner_rows(j, _):
        cols = aligned(j * share, share)
        values[EDGE:, cols] = inner(1, j) * inner(2, j)
        gate[EDGE:, cols] = inner(0, j)
        return 0

    lax.fori_loop(0, lanes, inner_rows, 0)
    edge.wait()

    def values_of(j):
        cols = aligned(j * share, share)
        values[0:EDGE, cols] = outer(1, j) * outer(2, j)
        return values[:, cols].T.astype(jnp.bfloat16)

    half = share // 2

    def values_copy(slot, peer, h):
        part = pl.ds(h * half, half)
        return pltpu.make_async_remote_copy(
            src_ref=send_v.at[peer, part],
            dst_ref=recv_v.at[behind + slot, part],
            send_sem=v_sems.at[h, peer],
            recv_sem=v_recvs.at[h, slot],
            device_id={"ctx": peer},
        )

    def far_first(i):
        k = lanes // 2 + (i + 1) // 2 * (2 * (i % 2) - 1)
        return lax.rem(me + k, lanes)

    def mixed_copy(slot, peer, h):
        part = pl.ds(h * half, half)
        return pltpu.make_async_remote_copy(
            src_ref=send_m.at[peer, part],
            dst_ref=recv_m.at[slot, part],
            send_sem=m_sems.at[h, peer],
            recv_sem=m_recvs.at[h, slot],
            device_id={"ctx": peer},
        )

    def send_values(i, _):
        peer = far_first(i)
        send_v[peer] = values_of(peer)
        values_copy(me, peer, 0).start()
        return 0

    def send_rest(i, _):
        values_copy(me, far_first(i), 1).start()
        return 0

    lax.fori_loop(0, lanes - 1, send_values, 0)
    lax.fori_loop(0, lanes - 1, send_rest, 0)
    recv_v[behind + me] = values_of(me)

    def gates(j, _):
        gate[0:EDGE, aligned(j * share, share)] = outer(0, j)
        return 0

    lax.fori_loop(0, lanes, gates, 0)

    def take_values(h):
        def take(i, _):
            peer = far_first(i)
            values_copy(peer, peer, h).wait_recv()
            return 0

        lax.fori_loop(0, lanes - 1, take, 0)

    def send_mixed(h):
        def start(i, _):
            mixed_copy(me, far_first(i), h).start()
            return 0

        lax.fori_loop(0, lanes - 1, start, 0)

    for g in range(own_groups):
        part = pl.ds(g * GSIZE, GSIZE)
        if g * GSIZE % half == 0:
            take_values(g * GSIZE // half)
        lhs = jnp.concatenate(
            [recv_v[b : b + lanes, part, :].reshape(lanes * GSIZE, rows) for b in range(behind + 1)],
            axis=1,
        )
        mixed = jnp.dot(lhs, toeplitz[g], preferred_element_type=jnp.float32)
        send_m[:, part, :] = mixed.astype(jnp.bfloat16).reshape(lanes, GSIZE, rows)
        if (g + 1) * GSIZE % half == 0:
            send_mixed(((g + 1) * GSIZE - 1) // half)

    recv_m[me] = send_m[me]

    def make_hidden(j):
        cols = aligned(j * share, share)
        mixed = recv_m[j].astype(jnp.float32).T
        hidden[:, cols] = (gate[:, cols] * mixed).astype(jnp.bfloat16)

    make_hidden(me)

    def take_mixed(i, _):
        peer = far_first(i)
        mixed_copy(peer, peer, 0).wait_recv()
        mixed_copy(peer, peer, 1).wait_recv()
        make_hidden(peer)
        return 0

    lax.fori_loop(0, lanes - 1, take_mixed, 0)
    loads[3].wait()

    def product(device, q):
        cols = aligned((device * pieces + q) * wide, wide)
        return jnp.dot(hidden[...], held_weight[:, cols], preferred_element_type=jnp.float32)

    def core_copy(dy, q):
        return pltpu.make_async_remote_copy(
            src_ref=core_send.at[dy, q],
            dst_ref=core_recv.at[dy, q],
            send_sem=cs_sems.at[dy, q],
            recv_sem=cr_sems.at[dy, q],
            device_id={"tp": partner},
        )

    def y_copy(dy, q):
        return pltpu.make_async_remote_copy(
            src_ref=y_send.at[dy, q],
            dst_ref=y_recv.at[dy, q],
            send_sem=ys_sems.at[dy, q],
            recv_sem=yr_sems.at[dy, q],
            device_id={"tp": lax.rem(y + dy, cores_y) * 2 + core},
        )

    for dy in list(range(1, cores_y)) + [0]:
        other = lax.rem(y + dy, cores_y) * 2

        def give(q, _):
            core_send[dy, q] = product(other + 1 - core, q).astype(jnp.bfloat16)
            core_copy(dy, q).start()
            return 0

        def add(q, _):
            mine = product(other + core, q)
            core_copy(dy, q).wait_recv()
            mine = mine + core_recv[dy, q].astype(jnp.float32)
            if dy:
                y_send[dy, q] = mine.astype(jnp.bfloat16)
                y_copy(dy, q).start()
            else:
                for other_dy in range(1, cores_y):
                    y_copy(other_dy, q).wait_recv()
                    mine = mine + y_recv[other_dy, q].astype(jnp.float32)
                out[:, aligned(q * wide, wide)] = mine.astype(jnp.bfloat16)
            return 0

        def both(q, _):
            give(q + 1, 0)
            return add(q, 0)

        if dy:
            give(0, 0)
            lax.fori_loop(0, pieces - 1, both, 0)
            add(pieces - 1, 0)
        else:
            lax.fori_loop(0, pieces, give, 0)
            lax.fori_loop(0, pieces, add, 0)

    def drain(k, _):
        peer = lax.rem(me + k, lanes)
        values_copy(me, peer, 0).wait_send()
        values_copy(me, peer, 1).wait_send()
        mixed_copy(me, peer, 0).wait_send()
        mixed_copy(me, peer, 1).wait_send()
        return 0

    lax.fori_loop(1, lanes, drain, 0)
    for dy in range(cores_y):

        def drain_sum(q, _):
            core_copy(dy, q).wait_send()
            if dy:
                y_copy(dy, q).wait_send()
            return 0

        lax.fori_loop(0, pieces, drain_sum, 0)


def fused(projected, short_filter, long_filter, out_weight):
    lanes, devices = lax.axis_size("ctx"), lax.axis_size("tp")
    rows, _, chans = projected.shape
    groups, reach = long_filter.shape
    features = out_weight.shape[1]
    cores_y = devices // 2
    share = chans // lanes
    behind = reach // rows
    own = features // devices
    pieces = 8
    wide = own // pieces
    bf16, f32 = jnp.bfloat16, jnp.float32
    vmem = pl.BlockSpec(memory_space=pltpu.VMEM)
    hbm = pl.BlockSpec(memory_space=pltpu.HBM)
    taps = short_filter.shape[0]
    dma = pltpu.SemaphoreType.DMA
    return pl.pallas_call(
        functools.partial(fused_kernel, lanes, cores_y),
        out_shape=pltpu.VMEM((rows, own), bf16),
        in_specs=[hbm] * 4,
        out_specs=vmem,
        scratch_shapes=[
            pltpu.VMEM((3, rows, chans), bf16),
            pltpu.VMEM((3, taps, chans), f32),
            pltpu.VMEM((groups, reach), bf16),
            pltpu.VMEM((chans, features), bf16),
            pltpu.VMEM((3, EDGE, chans), bf16),
            pltpu.VMEM((groups, reach + 2 * rows), f32),
            pltpu.VMEM((share // GSIZE, reach + rows, rows), bf16),
            pltpu.VMEM((rows, chans), f32),
            pltpu.VMEM((rows, chans), f32),
            pltpu.VMEM((lanes, share, rows), bf16),
            pltpu.VMEM((behind + lanes, share, rows), bf16),
            pltpu.VMEM((lanes, share, rows), bf16),
            pltpu.VMEM((lanes, share, rows), bf16),
            pltpu.VMEM((rows, chans), bf16),
            pltpu.VMEM((cores_y, pieces, rows, wide), bf16),
            pltpu.VMEM((cores_y, pieces, rows, wide), bf16),
            pltpu.VMEM((cores_y, pieces, rows, wide), bf16),
            pltpu.VMEM((cores_y, pieces, rows, wide), bf16),
            dma((4,)),
            dma((2,)),
            dma((2, lanes)),
            dma((2, lanes)),
            dma((2, lanes)),
            dma((2, lanes)),
            dma((cores_y, pieces)),
            dma((cores_y, pieces)),
            dma((cores_y, pieces)),
            dma((cores_y, pieces)),
        ],
        compiler_params=pltpu.CompilerParams(
            collective_id=0, has_side_effects=True, vmem_limit_bytes=62 * 2**20
        ),
        cost_estimate=pl.CostEstimate(
            flops=2 * rows * chans * features,
            bytes_accessed=2 * chans * features,
            transcendentals=0,
        ),
    )(jnp.transpose(projected, (1, 0, 2)), jnp.transpose(short_filter, (1, 0, 2)), long_filter, out_weight)


def fits(projected, long_filter, out_weight):
    lanes, devices = lax.axis_size("ctx"), lax.axis_size("tp")
    rows, _, chans = projected.shape
    share = chans // lanes
    return (
        rows % 128 == 0
        and share % 128 == 0
        and share * lanes == chans
        and lanes % 2 == 0
        and devices % 2 == 0
        and long_filter.shape[1] % rows == 0
        and out_weight.shape[1] % (devices * 1024) == 0
    )


def shifted(array, axis, by):
    size = lax.axis_size(axis)
    pairs = [(i, i + by) for i in range(size) if 0 <= i + by < size]
    return lax.ppermute(array, axis, pairs)


def toeplitz_block(padded_taps, lag_base, count, tok_rows):
    width = tok_rows + count - 1
    groups = padded_taps.shape[0]
    window = lax.dynamic_slice_in_dim(padded_taps, lag_base - (count - 1) + 2 * tok_rows, width, 1)
    flipped = jnp.concatenate([window[:, ::-1], jnp.zeros((groups, 1), window.dtype)], axis=1)
    tiled = jnp.tile(flipped, (1, tok_rows))
    skewed = tiled[:, : tok_rows * width].reshape(groups, tok_rows, width)
    return skewed[:, :, tok_rows - 1 : tok_rows - 1 + count]


def body(projected, short_filter, long_filter, out_weight):
    if fits(projected, long_filter, out_weight):
        return fused(projected, short_filter, long_filter, out_weight)
    tok_rows = projected.shape[0]
    taps = short_filter.shape[0]
    groups = long_filter.shape[0]
    reach = long_filter.shape[1]
    border = shifted(projected[tok_rows - (taps - 1) :], "ctx", 1)
    extended = jnp.concatenate([border, projected], axis=0).astype(jnp.float32)
    conved = short_filter[0] * extended[taps - 1 : taps - 1 + tok_rows]
    for offset in range(1, taps):
        conved = (
            conved
            + short_filter[offset] * extended[taps - 1 - offset : taps - 1 - offset + tok_rows]
        )
    values = (conved[:, 1, :] * conved[:, 2, :]).astype(jnp.bfloat16)
    padding = jnp.zeros((groups, 2 * tok_rows), long_filter.dtype)
    padded_taps = jnp.concatenate([padding, long_filter, padding], axis=1)
    lanes = lax.axis_size("ctx")
    whole = lax.all_to_all(values, "ctx", split_axis=1, concat_axis=0, tiled=True)
    share = whole.shape[1]
    held_groups = max(1, share // GSIZE)
    per_group = share // held_groups
    first_group = lax.axis_index("ctx") * share // GSIZE
    own_taps = lax.dynamic_slice_in_dim(padded_taps, first_group, held_groups, 0)
    behind = reach // tok_rows
    lead = jnp.zeros((behind * tok_rows, share), whole.dtype)
    stretched = jnp.concatenate([lead, whole], axis=0)
    blocks = stretched.reshape(behind + lanes, tok_rows, held_groups, per_group)

    def one_lag(step, total):
        matrix = toeplitz_block(own_taps, step * tok_rows, tok_rows, tok_rows)
        source = lax.dynamic_slice_in_dim(blocks, behind - step, lanes, 0)
        return total + jnp.einsum(
            "gts,osgi->otgi", matrix, source, preferred_element_type=jnp.float32
        )

    start_total = jnp.zeros((lanes, tok_rows, held_groups, per_group), jnp.float32)
    spread = lax.fori_loop(0, behind + 1, one_lag, start_total).reshape(lanes * tok_rows, share)
    mixed = lax.all_to_all(
        spread.astype(jnp.bfloat16), "ctx", split_axis=0, concat_axis=1, tiled=True
    ).astype(spread.dtype)
    hidden = (conved[:, 0, :] * mixed).astype(jnp.bfloat16)
    partial_sum = jnp.dot(hidden, out_weight, preferred_element_type=jnp.float32)
    return lax.psum_scatter(partial_sum.astype(jnp.bfloat16), "tp", scatter_dimension=1, tiled=True)


def solution(mesh):
    return jax.shard_map(
        body,
        mesh=mesh,
        in_specs=(P("ctx", None, "tp"), P(None, None, "tp"), P("tp", None), P("tp", None)),
        out_specs=P("ctx", "tp"),
        check_vma=False,
    )
```

```python
import functools

import jax
import jax.numpy as jnp
from jax import lax
from jax.experimental import pallas as pl
from jax.experimental.pallas import tpu as pltpu
from jax.sharding import PartitionSpec as P

GSIZE = 16
EDGE = 16


def aligned(start, size):
    return pl.ds(pl.multiple_of(start, size), size)


def fused_kernel(
    lanes,
    cores_y,
    proj_hbm,
    short_hbm,
    longf_hbm,
    weight,
    out,
    proj,
    short,
    longf,
    held_weight,
    border,
    padded,
    toeplitz,
    gate,
    values,
    send_v,
    recv_v,
    send_m,
    recv_m,
    hidden,
    core_send,
    core_recv,
    y_send,
    y_recv,
    load_sems,
    edge_sem,
    v_sems,
    v_recvs,
    m_sems,
    m_recvs,
    cs_sems,
    cr_sems,
    ys_sems,
    yr_sems,
):
    me = lax.axis_index("ctx")
    tp = lax.axis_index("tp")
    y, core = tp // 2, tp % 2
    partner = y * 2 + (1 - core)
    _, rows, chans = proj.shape
    taps = short.shape[1]
    reach = longf.shape[1]
    behind = reach // rows
    share = chans // lanes
    own_groups = share // GSIZE
    pieces, wide = y_send.shape[1], y_send.shape[3]

    loads = [
        pltpu.make_async_copy(source, target, load_sems.at[i])
        for i, (source, target) in enumerate(
            [(longf_hbm, longf), (proj_hbm, proj), (short_hbm, short), (weight, held_weight)]
        )
    ]
    for load in loads[:3]:
        load.start()

    barrier = pltpu.get_barrier_semaphore()
    for k in range(1, lanes):
        pl.semaphore_signal(barrier, inc=1, device_id={"ctx": lax.rem(me + k, lanes)})
    pl.semaphore_signal(barrier, inc=1, device_id={"tp": partner})
    for dy in range(1, cores_y):
        pl.semaphore_signal(
            barrier, inc=1, device_id={"tp": lax.rem(y + dy, cores_y) * 2 + core}
        )
    pl.semaphore_wait(barrier, lanes - 1 + 1 + cores_y - 1)

    edge = pltpu.make_async_remote_copy(
        src_ref=proj_hbm.at[:, pl.ds(rows - EDGE, EDGE), :],
        dst_ref=border,
        send_sem=edge_sem.at[0],
        recv_sem=edge_sem.at[1],
        device_id={"ctx": lax.rem(me + 1, lanes)},
    )
    edge.start()
    loads[0].wait()
    groups = longf.shape[0]
    padded[:, 0:rows] = jnp.zeros((groups, rows), jnp.float32)
    padded[:, rows : rows + reach] = longf[...].astype(jnp.float32)
    padded[:, rows + reach :] = jnp.zeros((groups, rows), jnp.float32)
    recv_v[0:behind] = jnp.zeros((behind, share, rows), jnp.bfloat16)

    def build(g, _):
        line = padded[pl.ds(me * own_groups + g, 1), :]
        flat = jnp.broadcast_to(line, (rows, reach + 2 * rows))
        skewed = pltpu.roll(flat, 0, 1, stride=1, stride_axis=0)
        for b in range(behind + 1):
            low = rows + reach - rows * b
            toeplitz[g, b * rows : (b + 1) * rows, :] = skewed[:, low : low + rows].astype(jnp.bfloat16)
        return 0

    lax.fori_loop(0, own_groups, build, 0, unroll=2)


    loads[1].wait()
    loads[2].wait()
    loads[3].start()

    def taps_over(ext, p, cols):
        total = short[p, 0:1, cols] * ext[EDGE:]
        for d in range(1, taps):
            total = total + short[p, d : d + 1, cols] * pltpu.roll(ext, d, 0)[EDGE:]
        return total

    def inner(p, j):
        return taps_over(proj[p, :, aligned(j * share, share)].astype(jnp.float32), p, aligned(j * share, share))

    def outer(p, j):
        cols = aligned(j * share, share)
        before = jnp.where(me == 0, 0.0, border[p, :, cols].astype(jnp.float32))
        first = proj[p, 0:EDGE, cols].astype(jnp.float32)
        return taps_over(jnp.concatenate([before, first], axis=0), p, cols)

    def inner_rows(j, _):
        cols = aligned(j * share, share)
        values[EDGE:, cols] = inner(1, j) * inner(2, j)
        gate[EDGE:, cols] = inner(0, j)
        return 0

    lax.fori_loop(0, lanes, inner_rows, 0, unroll=2)
    edge.wait()

    def values_of(j):
        cols = aligned(j * share, share)
        values[0:EDGE, cols] = outer(1, j) * outer(2, j)
        return values[:, cols].T.astype(jnp.bfloat16)

    half = share // 2

    def values_copy(slot, peer, h):
        part = pl.ds(h * half, half)
        return pltpu.make_async_remote_copy(
            src_ref=send_v.at[peer, part],
            dst_ref=recv_v.at[behind + slot, part],
            send_sem=v_sems.at[h, peer],
            recv_sem=v_recvs.at[h, slot],
            device_id={"ctx": peer},
        )

    def far_first(i):
        k = lanes // 2 + (i + 1) // 2 * (2 * (i % 2) - 1)
        return lax.rem(me + k, lanes)

    def mixed_copy(slot, peer, h):
        part = pl.ds(h * half, half)
        return pltpu.make_async_remote_copy(
            src_ref=send_m.at[peer, part],
            dst_ref=recv_m.at[slot, part],
            send_sem=m_sems.at[h, peer],
            recv_sem=m_recvs.at[h, slot],
            device_id={"ctx": peer},
        )

    def send_values(i, _):
        peer = far_first(i)
        send_v[peer] = values_of(peer)
        values_copy(me, peer, 0).start()
        return 0

    def send_rest(i, _):
        values_copy(me, far_first(i), 1).start()
        return 0

    lax.fori_loop(0, lanes - 1, send_values, 0)
    lax.fori_loop(0, lanes - 1, send_rest, 0)
    recv_v[behind + me] = values_of(me)

    def gates(j, _):
        gate[0:EDGE, aligned(j * share, share)] = outer(0, j)
        return 0

    lax.fori_loop(0, lanes, gates, 0)

    def take_values(h):
        def take(i, _):
            peer = far_first(i)
            values_copy(peer, peer, h).wait_recv()
            return 0

        lax.fori_loop(0, lanes - 1, take, 0)

    def send_mixed(h):
        def start(i, _):
            mixed_copy(me, far_first(i), h).start()
            return 0

        lax.fori_loop(0, lanes - 1, start, 0)

    for g in range(own_groups):
        part = pl.ds(g * GSIZE, GSIZE)
        if g * GSIZE % half == 0:
            take_values(g * GSIZE // half)
        lhs = jnp.concatenate(
            [recv_v[b : b + lanes, part, :].reshape(lanes * GSIZE, rows) for b in range(behind + 1)],
            axis=1,
        )
        mixed = jnp.dot(lhs, toeplitz[g], preferred_element_type=jnp.float32)
        send_m[:, part, :] = mixed.astype(jnp.bfloat16).reshape(lanes, GSIZE, rows)
        if (g + 1) * GSIZE % half == 0:
            send_mixed(((g + 1) * GSIZE - 1) // half)

    recv_m[me] = send_m[me]

    def make_hidden(j):
        cols = aligned(j * share, share)
        mixed = recv_m[j].astype(jnp.float32).T
        hidden[:, cols] = (gate[:, cols] * mixed).astype(jnp.bfloat16)

    make_hidden(me)

    def take_mixed(i, _):
        peer = far_first(i)
        mixed_copy(peer, peer, 0).wait_recv()
        mixed_copy(peer, peer, 1).wait_recv()
        make_hidden(peer)
        return 0

    lax.fori_loop(0, lanes - 1, take_mixed, 0)
    loads[3].wait()

    def product(device, q):
        cols = aligned((device * pieces + q) * wide, wide)
        return jnp.dot(hidden[...], held_weight[:, cols], preferred_element_type=jnp.float32)

    def core_copy(dy, q):
        return pltpu.make_async_remote_copy(
            src_ref=core_send.at[dy, q],
            dst_ref=core_recv.at[dy, q],
            send_sem=cs_sems.at[dy, q],
            recv_sem=cr_sems.at[dy, q],
            device_id={"tp": partner},
        )

    def y_copy(dy, q):
        return pltpu.make_async_remote_copy(
            src_ref=y_send.at[dy, q],
            dst_ref=y_recv.at[dy, q],
            send_sem=ys_sems.at[dy, q],
            recv_sem=yr_sems.at[dy, q],
            device_id={"tp": lax.rem(y + dy, cores_y) * 2 + core},
        )

    for dy in list(range(1, cores_y)) + [0]:
        other = lax.rem(y + dy, cores_y) * 2

        def give(q, _):
            core_send[dy, q] = product(other + 1 - core, q).astype(jnp.bfloat16)
            core_copy(dy, q).start()
            return 0

        def add(q, _):
            mine = product(other + core, q)
            core_copy(dy, q).wait_recv()
            mine = mine + core_recv[dy, q].astype(jnp.float32)
            if dy:
                y_send[dy, q] = mine.astype(jnp.bfloat16)
                y_copy(dy, q).start()
            else:
                for other_dy in range(1, cores_y):
                    y_copy(other_dy, q).wait_recv()
                    mine = mine + y_recv[other_dy, q].astype(jnp.float32)
                out[:, aligned(q * wide, wide)] = mine.astype(jnp.bfloat16)
            return 0

        def both(q, _):
            give(q + 1, 0)
            return add(q, 0)

        if dy:
            give(0, 0)
            lax.fori_loop(0, pieces - 1, both, 0)
            add(pieces - 1, 0)
        else:
            lax.fori_loop(0, pieces, give, 0)
            lax.fori_loop(0, pieces, add, 0)

    def drain(k, _):
        peer = lax.rem(me + k, lanes)
        values_copy(me, peer, 0).wait_send()
        values_copy(me, peer, 1).wait_send()
        mixed_copy(me, peer, 0).wait_send()
        mixed_copy(me, peer, 1).wait_send()
        return 0

    lax.fori_loop(1, lanes, drain, 0)
    for dy in range(cores_y):

        def drain_sum(q, _):
            core_copy(dy, q).wait_send()
            if dy:
                y_copy(dy, q).wait_send()
            return 0

        lax.fori_loop(0, pieces, drain_sum, 0)


def fused(projected, short_filter, long_filter, out_weight):
    lanes, devices = lax.axis_size("ctx"), lax.axis_size("tp")
    rows, _, chans = projected.shape
    groups, reach = long_filter.shape
    features = out_weight.shape[1]
    cores_y = devices // 2
    share = chans // lanes
    behind = reach // rows
    own = features // devices
    pieces = 8
    wide = own // pieces
    bf16, f32 = jnp.bfloat16, jnp.float32
    vmem = pl.BlockSpec(memory_space=pltpu.VMEM)
    hbm = pl.BlockSpec(memory_space=pltpu.HBM)
    taps = short_filter.shape[0]
    dma = pltpu.SemaphoreType.DMA
    return pl.pallas_call(
        functools.partial(fused_kernel, lanes, cores_y),
        out_shape=pltpu.VMEM((rows, own), bf16),
        in_specs=[hbm] * 4,
        out_specs=vmem,
        scratch_shapes=[
            pltpu.VMEM((3, rows, chans), bf16),
            pltpu.VMEM((3, taps, chans), f32),
            pltpu.VMEM((groups, reach), bf16),
            pltpu.VMEM((chans, features), bf16),
            pltpu.VMEM((3, EDGE, chans), bf16),
            pltpu.VMEM((groups, reach + 2 * rows), f32),
            pltpu.VMEM((share // GSIZE, reach + rows, rows), bf16),
            pltpu.VMEM((rows, chans), f32),
            pltpu.VMEM((rows, chans), f32),
            pltpu.VMEM((lanes, share, rows), bf16),
            pltpu.VMEM((behind + lanes, share, rows), bf16),
            pltpu.VMEM((lanes, share, rows), bf16),
            pltpu.VMEM((lanes, share, rows), bf16),
            pltpu.VMEM((rows, chans), bf16),
            pltpu.VMEM((cores_y, pieces, rows, wide), bf16),
            pltpu.VMEM((cores_y, pieces, rows, wide), bf16),
            pltpu.VMEM((cores_y, pieces, rows, wide), bf16),
            pltpu.VMEM((cores_y, pieces, rows, wide), bf16),
            dma((4,)),
            dma((2,)),
            dma((2, lanes)),
            dma((2, lanes)),
            dma((2, lanes)),
            dma((2, lanes)),
            dma((cores_y, pieces)),
            dma((cores_y, pieces)),
            dma((cores_y, pieces)),
            dma((cores_y, pieces)),
        ],
        compiler_params=pltpu.CompilerParams(
            collective_id=0, has_side_effects=True, vmem_limit_bytes=62 * 2**20
        ),
        cost_estimate=pl.CostEstimate(
            flops=2 * rows * chans * features,
            bytes_accessed=2 * chans * features,
            transcendentals=0,
        ),
    )(jnp.transpose(projected, (1, 0, 2)), jnp.transpose(short_filter, (1, 0, 2)), long_filter, out_weight)


def fits(projected, long_filter, out_weight):
    lanes, devices = lax.axis_size("ctx"), lax.axis_size("tp")
    rows, _, chans = projected.shape
    share = chans // lanes
    return (
        rows % 128 == 0
        and share % 128 == 0
        and share * lanes == chans
        and lanes % 2 == 0
        and devices % 2 == 0
        and long_filter.shape[1] % rows == 0
        and out_weight.shape[1] % (devices * 1024) == 0
    )


def shifted(array, axis, by):
    size = lax.axis_size(axis)
    pairs = [(i, i + by) for i in range(size) if 0 <= i + by < size]
    return lax.ppermute(array, axis, pairs)


def toeplitz_block(padded_taps, lag_base, count, tok_rows):
    width = tok_rows + count - 1
    groups = padded_taps.shape[0]
    window = lax.dynamic_slice_in_dim(padded_taps, lag_base - (count - 1) + 2 * tok_rows, width, 1)
    flipped = jnp.concatenate([window[:, ::-1], jnp.zeros((groups, 1), window.dtype)], axis=1)
    tiled = jnp.tile(flipped, (1, tok_rows))
    skewed = tiled[:, : tok_rows * width].reshape(groups, tok_rows, width)
    return skewed[:, :, tok_rows - 1 : tok_rows - 1 + count]


def body(projected, short_filter, long_filter, out_weight):
    if fits(projected, long_filter, out_weight):
        return fused(projected, short_filter, long_filter, out_weight)
    tok_rows = projected.shape[0]
    taps = short_filter.shape[0]
    groups = long_filter.shape[0]
    reach = long_filter.shape[1]
    border = shifted(projected[tok_rows - (taps - 1) :], "ctx", 1)
    extended = jnp.concatenate([border, projected], axis=0).astype(jnp.float32)
    conved = short_filter[0] * extended[taps - 1 : taps - 1 + tok_rows]
    for offset in range(1, taps):
        conved = (
            conved
            + short_filter[offset] * extended[taps - 1 - offset : taps - 1 - offset + tok_rows]
        )
    values = (conved[:, 1, :] * conved[:, 2, :]).astype(jnp.bfloat16)
    padding = jnp.zeros((groups, 2 * tok_rows), long_filter.dtype)
    padded_taps = jnp.concatenate([padding, long_filter, padding], axis=1)
    lanes = lax.axis_size("ctx")
    whole = lax.all_to_all(values, "ctx", split_axis=1, concat_axis=0, tiled=True)
    share = whole.shape[1]
    held_groups = max(1, share // GSIZE)
    per_group = share // held_groups
    first_group = lax.axis_index("ctx") * share // GSIZE
    own_taps = lax.dynamic_slice_in_dim(padded_taps, first_group, held_groups, 0)
    behind = reach // tok_rows
    lead = jnp.zeros((behind * tok_rows, share), whole.dtype)
    stretched = jnp.concatenate([lead, whole], axis=0)
    blocks = stretched.reshape(behind + lanes, tok_rows, held_groups, per_group)

    def one_lag(step, total):
        matrix = toeplitz_block(own_taps, step * tok_rows, tok_rows, tok_rows)
        source = lax.dynamic_slice_in_dim(blocks, behind - step, lanes, 0)
        return total + jnp.einsum(
            "gts,osgi->otgi", matrix, source, preferred_element_type=jnp.float32
        )

    start_total = jnp.zeros((lanes, tok_rows, held_groups, per_group), jnp.float32)
    spread = lax.fori_loop(0, behind + 1, one_lag, start_total).reshape(lanes * tok_rows, share)
    mixed = lax.all_to_all(
        spread.astype(jnp.bfloat16), "ctx", split_axis=0, concat_axis=1, tiled=True
    ).astype(spread.dtype)
    hidden = (conved[:, 0, :] * mixed).astype(jnp.bfloat16)
    partial_sum = jnp.dot(hidden, out_weight, preferred_element_type=jnp.float32)
    return lax.psum_scatter(partial_sum.astype(jnp.bfloat16), "tp", scatter_dimension=1, tiled=True)


def solution(mesh):
    return jax.shard_map(
        body,
        mesh=mesh,
        in_specs=(P("ctx", None, "tp"), P(None, None, "tp"), P("tp", None), P("tp", None)),
        out_specs=P("ctx", "tp"),
        check_vma=False,
    )
```

```python
import functools

import jax
import jax.numpy as jnp
from jax import lax
from jax.experimental import pallas as pl
from jax.experimental.pallas import tpu as pltpu
from jax.sharding import PartitionSpec as P

GSIZE = 16
EDGE = 16


def aligned(start, size):
    return pl.ds(pl.multiple_of(start, size), size)


def fused_kernel(
    lanes,
    cores_y,
    proj_hbm,
    short_hbm,
    longf_hbm,
    weight,
    out,
    proj,
    short,
    longf,
    held_weight,
    border,
    padded,
    toeplitz,
    gate,
    values,
    send_v,
    recv_v,
    send_m,
    recv_m,
    hidden,
    core_send,
    core_recv,
    y_send,
    y_recv,
    load_sems,
    edge_sem,
    v_sems,
    v_recvs,
    m_sems,
    m_recvs,
    cs_sems,
    cr_sems,
    ys_sems,
    yr_sems,
):
    me = lax.axis_index("ctx")
    tp = lax.axis_index("tp")
    y, core = tp // 2, tp % 2
    partner = y * 2 + (1 - core)
    _, rows, chans = proj.shape
    taps = short.shape[1]
    reach = longf.shape[1]
    behind = reach // rows
    share = chans // lanes
    own_groups = share // GSIZE
    pieces, wide = y_send.shape[1], y_send.shape[3]

    loads = [
        pltpu.make_async_copy(source, target, load_sems.at[i])
        for i, (source, target) in enumerate(
            [(longf_hbm, longf), (proj_hbm, proj), (short_hbm, short), (weight, held_weight)]
        )
    ]
    for load in loads[:3]:
        load.start()

    barrier = pltpu.get_barrier_semaphore()
    for k in range(1, lanes):
        pl.semaphore_signal(barrier, inc=1, device_id={"ctx": lax.rem(me + k, lanes)})
    pl.semaphore_signal(barrier, inc=1, device_id={"tp": partner})
    for dy in range(1, cores_y):
        pl.semaphore_signal(
            barrier, inc=1, device_id={"tp": lax.rem(y + dy, cores_y) * 2 + core}
        )
    pl.semaphore_wait(barrier, lanes - 1 + 1 + cores_y - 1)

    edge = pltpu.make_async_remote_copy(
        src_ref=proj_hbm.at[:, pl.ds(rows - EDGE, EDGE), :],
        dst_ref=border,
        send_sem=edge_sem.at[0],
        recv_sem=edge_sem.at[1],
        device_id={"ctx": lax.rem(me + 1, lanes)},
    )
    edge.start()
    loads[0].wait()
    groups = longf.shape[0]
    padded[:, 0:rows] = jnp.zeros((groups, rows), jnp.float32)
    padded[:, rows : rows + reach] = longf[...].astype(jnp.float32)
    padded[:, rows + reach :] = jnp.zeros((groups, rows), jnp.float32)
    recv_v[0:behind] = jnp.zeros((behind, share, rows), jnp.bfloat16)

    def build(g, _):
        line = padded[pl.ds(me * own_groups + g, 1), :]
        flat = jnp.broadcast_to(line, (rows, reach + 2 * rows))
        skewed = pltpu.roll(flat, 0, 1, stride=1, stride_axis=0)
        for b in range(behind + 1):
            low = rows + reach - rows * b
            toeplitz[g, b * rows : (b + 1) * rows, :] = skewed[:, low : low + rows].astype(jnp.bfloat16)
        return 0

    lax.fori_loop(0, own_groups, build, 0, unroll=2)


    loads[1].wait()
    loads[2].wait()
    loads[3].start()

    def taps_over(ext, p, cols):
        total = short[p, 0:1, cols] * ext[EDGE:]
        for d in range(1, taps):
            total = total + short[p, d : d + 1, cols] * pltpu.roll(ext, d, 0)[EDGE:]
        return total

    def inner(p, j):
        return taps_over(proj[p, :, aligned(j * share, share)].astype(jnp.float32), p, aligned(j * share, share))

    def outer(p, j):
        cols = aligned(j * share, share)
        before = jnp.where(me == 0, 0.0, border[p, :, cols].astype(jnp.float32))
        first = proj[p, 0:EDGE, cols].astype(jnp.float32)
        return taps_over(jnp.concatenate([before, first], axis=0), p, cols)

    def inner_rows(j, _):
        cols = aligned(j * share, share)
        values[EDGE:, cols] = inner(1, j) * inner(2, j)
        gate[EDGE:, cols] = inner(0, j)
        return 0

    lax.fori_loop(0, lanes, inner_rows, 0, unroll=2)
    edge.wait()

    def values_of(j):
        cols = aligned(j * share, share)
        values[0:EDGE, cols] = outer(1, j) * outer(2, j)
        return values[:, cols].T.astype(jnp.bfloat16)

    half = share // 2

    def values_copy(slot, peer, h):
        part = pl.ds(h * half, half)
        return pltpu.make_async_remote_copy(
            src_ref=send_v.at[peer, part],
            dst_ref=recv_v.at[behind + slot, part],
            send_sem=v_sems.at[h, peer],
            recv_sem=v_recvs.at[h, slot],
            device_id={"ctx": peer},
        )

    def far_first(i):
        k = lanes // 2 + (i + 1) // 2 * (2 * (i % 2) - 1)
        return lax.rem(me + k, lanes)

    def mixed_copy(slot, peer, h):
        part = pl.ds(h * half, half)
        return pltpu.make_async_remote_copy(
            src_ref=send_m.at[peer, part],
            dst_ref=recv_m.at[slot, part],
            send_sem=m_sems.at[h, peer],
            recv_sem=m_recvs.at[h, slot],
            device_id={"ctx": peer},
        )

    def send_values(i, _):
        peer = far_first(i)
        send_v[peer] = values_of(peer)
        values_copy(me, peer, 0).start()
        return 0

    def send_rest(i, _):
        values_copy(me, far_first(i), 1).start()
        return 0

    lax.fori_loop(0, lanes - 1, send_values, 0, unroll=True)
    lax.fori_loop(0, lanes - 1, send_rest, 0)
    recv_v[behind + me] = values_of(me)

    def gates(j, _):
        gate[0:EDGE, aligned(j * share, share)] = outer(0, j)
        return 0

    lax.fori_loop(0, lanes, gates, 0, unroll=2)

    def take_values(h):
        def take(i, _):
            peer = far_first(i)
            values_copy(peer, peer, h).wait_recv()
            return 0

        lax.fori_loop(0, lanes - 1, take, 0)

    def send_mixed(h):
        def start(i, _):
            mixed_copy(me, far_first(i), h).start()
            return 0

        lax.fori_loop(0, lanes - 1, start, 0)

    for g in range(own_groups):
        part = pl.ds(g * GSIZE, GSIZE)
        if g * GSIZE % half == 0:
            take_values(g * GSIZE // half)
        lhs = jnp.concatenate(
            [recv_v[b : b + lanes, part, :].reshape(lanes * GSIZE, rows) for b in range(behind + 1)],
            axis=1,
        )
        mixed = jnp.dot(lhs, toeplitz[g], preferred_element_type=jnp.float32)
        send_m[:, part, :] = mixed.astype(jnp.bfloat16).reshape(lanes, GSIZE, rows)
        if (g + 1) * GSIZE % half == 0:
            send_mixed(((g + 1) * GSIZE - 1) // half)

    recv_m[me] = send_m[me]

    def make_hidden(j):
        cols = aligned(j * share, share)
        mixed = recv_m[j].astype(jnp.float32).T
        hidden[:, cols] = (gate[:, cols] * mixed).astype(jnp.bfloat16)

    make_hidden(me)

    def take_mixed(i, _):
        peer = far_first(i)
        mixed_copy(peer, peer, 0).wait_recv()
        mixed_copy(peer, peer, 1).wait_recv()
        make_hidden(peer)
        return 0

    lax.fori_loop(0, lanes - 1, take_mixed, 0)
    loads[3].wait()

    def product(device, q):
        cols = aligned((device * pieces + q) * wide, wide)
        return jnp.dot(hidden[...], held_weight[:, cols], preferred_element_type=jnp.float32)

    def core_copy(dy, q):
        return pltpu.make_async_remote_copy(
            src_ref=core_send.at[dy, q],
            dst_ref=core_recv.at[dy, q],
            send_sem=cs_sems.at[dy, q],
            recv_sem=cr_sems.at[dy, q],
            device_id={"tp": partner},
        )

    def y_copy(dy, q):
        return pltpu.make_async_remote_copy(
            src_ref=y_send.at[dy, q],
            dst_ref=y_recv.at[dy, q],
            send_sem=ys_sems.at[dy, q],
            recv_sem=yr_sems.at[dy, q],
            device_id={"tp": lax.rem(y + dy, cores_y) * 2 + core},
        )

    for dy in list(range(1, cores_y)) + [0]:
        other = lax.rem(y + dy, cores_y) * 2

        def give(q, _):
            core_send[dy, q] = product(other + 1 - core, q).astype(jnp.bfloat16)
            core_copy(dy, q).start()
            return 0

        def add(q, _):
            mine = product(other + core, q)
            core_copy(dy, q).wait_recv()
            mine = mine + core_recv[dy, q].astype(jnp.float32)
            if dy:
                y_send[dy, q] = mine.astype(jnp.bfloat16)
                y_copy(dy, q).start()
            else:
                for other_dy in range(1, cores_y):
                    y_copy(other_dy, q).wait_recv()
                    mine = mine + y_recv[other_dy, q].astype(jnp.float32)
                out[:, aligned(q * wide, wide)] = mine.astype(jnp.bfloat16)
            return 0

        def both(q, _):
            give(q + 1, 0)
            return add(q, 0)

        if dy:
            give(0, 0)
            lax.fori_loop(0, pieces - 1, both, 0)
            add(pieces - 1, 0)
        else:
            lax.fori_loop(0, pieces, give, 0)
            lax.fori_loop(0, pieces, add, 0)

    def drain(k, _):
        peer = lax.rem(me + k, lanes)
        values_copy(me, peer, 0).wait_send()
        values_copy(me, peer, 1).wait_send()
        mixed_copy(me, peer, 0).wait_send()
        mixed_copy(me, peer, 1).wait_send()
        return 0

    lax.fori_loop(1, lanes, drain, 0)
    for dy in range(cores_y):

        def drain_sum(q, _):
            core_copy(dy, q).wait_send()
            if dy:
                y_copy(dy, q).wait_send()
            return 0

        lax.fori_loop(0, pieces, drain_sum, 0)


def fused(projected, short_filter, long_filter, out_weight):
    lanes, devices = lax.axis_size("ctx"), lax.axis_size("tp")
    rows, _, chans = projected.shape
    groups, reach = long_filter.shape
    features = out_weight.shape[1]
    cores_y = devices // 2
    share = chans // lanes
    behind = reach // rows
    own = features // devices
    pieces = 8
    wide = own // pieces
    bf16, f32 = jnp.bfloat16, jnp.float32
    vmem = pl.BlockSpec(memory_space=pltpu.VMEM)
    hbm = pl.BlockSpec(memory_space=pltpu.HBM)
    taps = short_filter.shape[0]
    dma = pltpu.SemaphoreType.DMA
    return pl.pallas_call(
        functools.partial(fused_kernel, lanes, cores_y),
        out_shape=pltpu.VMEM((rows, own), bf16),
        in_specs=[hbm] * 4,
        out_specs=vmem,
        scratch_shapes=[
            pltpu.VMEM((3, rows, chans), bf16),
            pltpu.VMEM((3, taps, chans), f32),
            pltpu.VMEM((groups, reach), bf16),
            pltpu.VMEM((chans, features), bf16),
            pltpu.VMEM((3, EDGE, chans), bf16),
            pltpu.VMEM((groups, reach + 2 * rows), f32),
            pltpu.VMEM((share // GSIZE, reach + rows, rows), bf16),
            pltpu.VMEM((rows, chans), f32),
            pltpu.VMEM((rows, chans), f32),
            pltpu.VMEM((lanes, share, rows), bf16),
            pltpu.VMEM((behind + lanes, share, rows), bf16),
            pltpu.VMEM((lanes, share, rows), bf16),
            pltpu.VMEM((lanes, share, rows), bf16),
            pltpu.VMEM((rows, chans), bf16),
            pltpu.VMEM((cores_y, pieces, rows, wide), bf16),
            pltpu.VMEM((cores_y, pieces, rows, wide), bf16),
            pltpu.VMEM((cores_y, pieces, rows, wide), bf16),
            pltpu.VMEM((cores_y, pieces, rows, wide), bf16),
            dma((4,)),
            dma((2,)),
            dma((2, lanes)),
            dma((2, lanes)),
            dma((2, lanes)),
            dma((2, lanes)),
            dma((cores_y, pieces)),
            dma((cores_y, pieces)),
            dma((cores_y, pieces)),
            dma((cores_y, pieces)),
        ],
        compiler_params=pltpu.CompilerParams(
            collective_id=0, has_side_effects=True, vmem_limit_bytes=62 * 2**20
        ),
        cost_estimate=pl.CostEstimate(
            flops=2 * rows * chans * features,
            bytes_accessed=2 * chans * features,
            transcendentals=0,
        ),
    )(jnp.transpose(projected, (1, 0, 2)), jnp.transpose(short_filter, (1, 0, 2)), long_filter, out_weight)


def fits(projected, long_filter, out_weight):
    lanes, devices = lax.axis_size("ctx"), lax.axis_size("tp")
    rows, _, chans = projected.shape
    share = chans // lanes
    return (
        rows % 128 == 0
        and share % 128 == 0
        and share * lanes == chans
        and lanes % 2 == 0
        and devices % 2 == 0
        and long_filter.shape[1] % rows == 0
        and out_weight.shape[1] % (devices * 1024) == 0
    )


def shifted(array, axis, by):
    size = lax.axis_size(axis)
    pairs = [(i, i + by) for i in range(size) if 0 <= i + by < size]
    return lax.ppermute(array, axis, pairs)


def toeplitz_block(padded_taps, lag_base, count, tok_rows):
    width = tok_rows + count - 1
    groups = padded_taps.shape[0]
    window = lax.dynamic_slice_in_dim(padded_taps, lag_base - (count - 1) + 2 * tok_rows, width, 1)
    flipped = jnp.concatenate([window[:, ::-1], jnp.zeros((groups, 1), window.dtype)], axis=1)
    tiled = jnp.tile(flipped, (1, tok_rows))
    skewed = tiled[:, : tok_rows * width].reshape(groups, tok_rows, width)
    return skewed[:, :, tok_rows - 1 : tok_rows - 1 + count]


def body(projected, short_filter, long_filter, out_weight):
    if fits(projected, long_filter, out_weight):
        return fused(projected, short_filter, long_filter, out_weight)
    tok_rows = projected.shape[0]
    taps = short_filter.shape[0]
    groups = long_filter.shape[0]
    reach = long_filter.shape[1]
    border = shifted(projected[tok_rows - (taps - 1) :], "ctx", 1)
    extended = jnp.concatenate([border, projected], axis=0).astype(jnp.float32)
    conved = short_filter[0] * extended[taps - 1 : taps - 1 + tok_rows]
    for offset in range(1, taps):
        conved = (
            conved
            + short_filter[offset] * extended[taps - 1 - offset : taps - 1 - offset + tok_rows]
        )
    values = (conved[:, 1, :] * conved[:, 2, :]).astype(jnp.bfloat16)
    padding = jnp.zeros((groups, 2 * tok_rows), long_filter.dtype)
    padded_taps = jnp.concatenate([padding, long_filter, padding], axis=1)
    lanes = lax.axis_size("ctx")
    whole = lax.all_to_all(values, "ctx", split_axis=1, concat_axis=0, tiled=True)
    share = whole.shape[1]
    held_groups = max(1, share // GSIZE)
    per_group = share // held_groups
    first_group = lax.axis_index("ctx") * share // GSIZE
    own_taps = lax.dynamic_slice_in_dim(padded_taps, first_group, held_groups, 0)
    behind = reach // tok_rows
    lead = jnp.zeros((behind * tok_rows, share), whole.dtype)
    stretched = jnp.concatenate([lead, whole], axis=0)
    blocks = stretched.reshape(behind + lanes, tok_rows, held_groups, per_group)

    def one_lag(step, total):
        matrix = toeplitz_block(own_taps, step * tok_rows, tok_rows, tok_rows)
        source = lax.dynamic_slice_in_dim(blocks, behind - step, lanes, 0)
        return total + jnp.einsum(
            "gts,osgi->otgi", matrix, source, preferred_element_type=jnp.float32
        )

    start_total = jnp.zeros((lanes, tok_rows, held_groups, per_group), jnp.float32)
    spread = lax.fori_loop(0, behind + 1, one_lag, start_total).reshape(lanes * tok_rows, share)
    mixed = lax.all_to_all(
        spread.astype(jnp.bfloat16), "ctx", split_axis=0, concat_axis=1, tiled=True
    ).astype(spread.dtype)
    hidden = (conved[:, 0, :] * mixed).astype(jnp.bfloat16)
    partial_sum = jnp.dot(hidden, out_weight, preferred_element_type=jnp.float32)
    return lax.psum_scatter(partial_sum.astype(jnp.bfloat16), "tp", scatter_dimension=1, tiled=True)


def solution(mesh):
    return jax.shard_map(
        body,
        mesh=mesh,
        in_specs=(P("ctx", None, "tp"), P(None, None, "tp"), P("tp", None), P("tp", None)),
        out_specs=P("ctx", "tp"),
        check_vma=False,
    )
```
